256 devices in a mesh: grp: 16 (over z_hi, y), dev: 16 (over x, z_lo, core).
Axes of the slice: x: 4, y: 4, z: 8 (z_hi: 4, z_lo: 2; z = z_hi * 2 + z_lo), core: 2. Of those that a mesh axis runs over, the one named last changes fastest.
Arguments:
- features: bfloat16 [8192, 32, 768], P(('grp', 'dev'))
- teacher: bfloat16 [8192, 1024], P(('grp', 'dev'))
- gain: float32 [768], replicated, may hold values from 0.25 to 1.75
- w_head: bfloat16 [768, 1024], replicated
- positives: int32 [8192], P(('grp', 'dev')), may hold values from 0 to 8191, as said below
Outputs:
- loss: float32 [], replicated
- grad_features: bfloat16 [8192, 32, 768], P(('grp', 'dev'))
- grad_head: float32 [768, 1024], P('grp', 'dev')
- grad_gain: float32 [768], replicated
The draws below stay inside these ranges and needn't reach their ends.
Inputs may be any that keep to these rules, and one draw needn't show every extreme that they name: `positives`: every teacher row is the positive of exactly one variant.
All inputs are finite; a program needn't handle non-finite values.
Results may differ from the reference program's by a relative error of at most 0.0061.
Values may be sent and summed in bfloat16 or wider, within the bound.
No kernel may reach another device: no remote copies, remote signals or barrier semaphores. Data moves between devices by JAX's collectives and lax.ppermute only.
A program may use at most 64 MiB of HBM per device.

```python
import jax
import jax.numpy as jnp
from jax import lax

D = 768
E = 1024
WIN = 32
N = 8192
N_GRP = 16


def shared_parts(key):
    latent = jax.random.normal(jax.random.fold_in(key, 101), (N, D), jnp.float32)
    head = jax.random.normal(jax.random.fold_in(key, 102), (D, E), jnp.float32) * D ** (-0.5)
    order = jax.random.permutation(jax.random.fold_in(key, 103), N).astype(jnp.int32)
    return (latent, head, order)


def draw_positives(key, part):
    latent, head, order = shared_parts(key)
    return order


def draw_w_head(key, part):
    latent, head, order = shared_parts(key)
    return head.astype(jnp.bfloat16)


def draw_features(key, part):
    latent, head, order = shared_parts(key)
    key = jax.random.fold_in(key, 13)
    noise = jax.random.normal(key, (N, WIN, D), jnp.float32)
    return (latent[:, None, :] + noise).astype(jnp.bfloat16)


def draw_teacher(key, part):
    latent, head, order = shared_parts(key)
    key = jax.random.fold_in(key, 14)
    ramp = jnp.arange(N, dtype=jnp.float32) / (N - 1)
    projected = jnp.dot(latent, head, precision=lax.Precision.HIGHEST)
    strength = 0.02 + 0.13 * ramp
    noise = jax.random.normal(key, (N, E), jnp.float32)
    rows = strength[:, None] * projected + noise
    teacher = jnp.zeros((N, E), jnp.float32).at[order].set(rows)
    return teacher.astype(jnp.bfloat16)


def setup_inputs(seed: int = 0) -> dict:
    keys = jax.random.split(jax.random.key(seed), 6)
    return {
        "features": draw_features(jax.random.fold_in(keys[5], 71), 0),
        "teacher": draw_teacher(jax.random.fold_in(keys[5], 71), 0),
        "gain": jnp.clip(1.0 + 0.15 * jax.random.normal(keys[2], (D,), jnp.float32), 0.25, 1.75),
        "w_head": draw_w_head(jax.random.fold_in(keys[5], 71), 0),
        "positives": draw_positives(jax.random.fold_in(keys[5], 71), 0),
    }


logit_scale = 64.0
norm_eps = 1e-06

def rms_scale(pooled, gain):
    radius = jnp.sqrt(lax.optimization_barrier(jnp.mean(pooled * pooled, axis=-1, keepdims=True)) + norm_eps)
    return pooled / radius * gain

def unit_rows(raw):
    length = jnp.sqrt(lax.optimization_barrier(jnp.sum(raw * raw, axis=-1, keepdims=True)) + norm_eps)
    return (raw / length, length)

def reference(features, teacher, gain, w_head, positives):
    total = teacher.shape[0]
    pooled = lax.optimization_barrier(jnp.mean(features, axis=1, dtype=jnp.float32))
    normed = rms_scale(pooled, gain).astype(jnp.bfloat16)
    raw = jnp.dot(normed, w_head, preferred_element_type=jnp.float32)
    unit, length = unit_rows(raw)
    student = unit.astype(jnp.bfloat16)
    teacher_unit = unit_rows(teacher.astype(jnp.float32))[0].astype(jnp.bfloat16)
    blocks = student.reshape(N_GRP, -1, student.shape[1])
    pos_blocks = positives.reshape(N_GRP, -1)
    column_ids = jnp.arange(total, dtype=jnp.int32)

    def first_pass(col_acc, item):
        rows_block, pos_block = item
        scores = logit_scale * jnp.dot(rows_block, teacher_unit.T, preferred_element_type=jnp.float32)
        expo = jnp.exp(scores)
        mask = (column_ids[None, :] == pos_block[:, None]).astype(jnp.float32)
        return (col_acc + lax.optimization_barrier(jnp.sum(expo, axis=0)), (lax.optimization_barrier(jnp.sum(expo, axis=1)), jnp.sum(scores * mask)))
    col_sums, (row_sums, pos_scores) = lax.scan(first_pass, jnp.zeros((total,), jnp.float32), (blocks, pos_blocks))
    loss = (jnp.sum(jnp.log(row_sums)) + jnp.sum(jnp.log(col_sums)) - 2.0 * jnp.sum(pos_scores)) / (2.0 * total)

    def second_pass(item):
        rows_block, pos_block, block_sums = item
        scores = logit_scale * jnp.dot(rows_block, teacher_unit.T, preferred_element_type=jnp.float32)
        expo = jnp.exp(scores)
        mask = (column_ids[None, :] == pos_block[:, None]).astype(jnp.float32)
        weights = (expo / block_sums[:, None] + expo / col_sums[None, :] - 2.0 * mask).astype(jnp.bfloat16)
        return logit_scale * jnp.dot(weights, teacher_unit, preferred_element_type=jnp.float32)
    grad_unit = lax.map(second_pass, (blocks, pos_blocks, row_sums)).reshape(total, -1)
    along = lax.optimization_barrier(jnp.sum(unit * grad_unit, axis=-1, keepdims=True))
    grad_raw = ((grad_unit - unit * along) / length).astype(jnp.bfloat16)
    grad_head = jnp.dot(normed.T, grad_raw, preferred_element_type=jnp.float32)
    grad_normed = jnp.dot(grad_raw, w_head.T, preferred_element_type=jnp.float32)
    radius = jnp.sqrt(lax.optimization_barrier(jnp.mean(pooled * pooled, axis=-1, keepdims=True)) + norm_eps)
    grad_gain = lax.optimization_barrier(jnp.sum(grad_normed * pooled / radius, axis=0))
    _, pullback = jax.vjp(lambda value: rms_scale(value, gain), pooled)
    grad_pooled = pullback(grad_normed)[0]
    window = features.shape[1]
    grad_features = jnp.broadcast_to((grad_pooled / window)[:, None, :], features.shape).astype(jnp.bfloat16)
    return (loss, grad_features, grad_head, grad_gain)
```

```python
import jax
import jax.numpy as jnp
from jax import lax
from jax.sharding import Mesh, PartitionSpec as P

logit_scale = 64.0
norm_eps = 1e-06

AXES = ("zh", "y", "x", "zl", "c")
ROW = ("y", "x")
COL = ("zh", "zl", "c")


def unit_rows(raw):
    length = jnp.sqrt(jnp.sum(raw * raw, axis=-1, keepdims=True) + norm_eps)
    return (raw / length, length)


def swap(blocks, axes):
    return lax.all_to_all(blocks, axes, 0, 0, tiled=True)


def spread(block, axes):
    peers = lax.axis_size(axes)
    return swap(jnp.broadcast_to(block[None], (peers,) + block.shape), axes)


def halves(value):
    high = value.astype(jnp.bfloat16)
    return high, (value - high.astype(jnp.float32)).astype(jnp.bfloat16)


def body(features, teacher, gain, w_head, positives):
    f32, b16 = jnp.float32, jnp.bfloat16
    rows, width = teacher.shape
    depth, window = features.shape[2], features.shape[1]
    nzh, ny, nx, nzl, nc = (lax.axis_size(a) for a in AXES)
    nrow, ncol = ny * nx, nzh * nzl * nc
    devices = nrow * ncol
    total = rows * devices
    part_rows, part_cols = depth // (nzh * ny), width // (nx * nzl * nc)

    teacher_unit = unit_rows(teacher.astype(f32))[0].astype(b16)
    columns = spread(teacher_unit, COL).reshape(ncol * rows, width)

    pooled = jnp.mean(features, axis=1, dtype=f32)
    radius = jnp.sqrt(jnp.mean(pooled * pooled, axis=-1, keepdims=True) + norm_eps)
    scaled = pooled / radius
    normed = (scaled * gain).astype(b16)
    raw = jnp.dot(normed, w_head, preferred_element_type=f32)
    unit, length = unit_rows(raw)
    student = unit.astype(b16)

    share = normed.reshape(rows, nzh, ny, part_rows).transpose(2, 0, 1, 3)
    share = share.reshape(ny, 1, rows, nzh * part_rows)
    share = jnp.broadcast_to(share, (ny, nx) + share.shape[2:]).reshape(nrow, rows, -1)
    pad = 64
    marks = jnp.stack([positives // 128, positives % 128], axis=1).astype(b16)
    marks = jnp.pad(marks, ((0, 0), (0, pad - 2)))
    same = lambda a: jnp.broadcast_to(a[None], (nrow,) + a.shape)
    sent = jnp.concatenate([same(student), share, same(marks)], axis=2)
    got = swap(sent, ROW).reshape(nrow * rows, -1)
    students = got[:, :width]
    normed_rows = got[:, width : width + nzh * part_rows]
    marks = got[:, width + nzh * part_rows :][:, :2].astype(jnp.int32)
    wanted = marks[:, 0] * 128 + marks[:, 1]

    place = jnp.arange(ncol * rows, dtype=jnp.int32)
    peer, inner = place // rows, place % rows
    pzh, pzl, pc = peer // (nzl * nc), (peer // nc) % nzl, peer % nc
    flat = (((pzh * ny + lax.axis_index("y")) * nx + lax.axis_index("x")) * nzl + pzl) * nc + pc
    column_ids = flat * rows + inner

    scores = logit_scale * jnp.dot(students, columns.T, preferred_element_type=f32)
    expo = jnp.exp(scores)
    mask = (column_ids[None, :] == wanted[:, None]).astype(f32)
    row_part = jnp.sum(expo, axis=1)
    col_part = jnp.sum(expo, axis=0)
    pos_part = jnp.sum(scores * mask)
    row_sums = jnp.sum(spread(row_part, ROW), axis=0)
    col_sums = jnp.sum(spread(col_part, COL), axis=0)
    loss_part = (
        jnp.sum(jnp.log(row_sums)) / nrow + jnp.sum(jnp.log(col_sums)) / ncol - 2.0 * pos_part
    )

    weights = (expo / row_sums[:, None] + expo / col_sums[None, :] - 2.0 * mask).astype(b16)
    terms = jnp.dot(weights, columns, preferred_element_type=f32).astype(b16)
    terms = swap(terms.reshape(nrow, rows, width), ROW)
    grad_unit = logit_scale * jnp.sum(terms.astype(f32), axis=0)
    along = jnp.sum(unit * grad_unit, axis=-1, keepdims=True)
    grad_raw = ((grad_unit - unit * along) / length).astype(b16)
    grad_normed = jnp.dot(grad_raw, w_head.T, preferred_element_type=f32)
    gain_part = jnp.sum(grad_normed * scaled, axis=0)

    wide = width // nx
    pieces = grad_raw.reshape(rows, nx, wide).transpose(1, 0, 2)
    pieces = jnp.broadcast_to(pieces[None], (ny,) + pieces.shape).reshape(nrow, rows, wide)
    extra = jnp.concatenate([gain_part, loss_part[None], jnp.zeros((255,), f32)])
    extra = jnp.concatenate(halves(extra)).reshape(-1, wide)
    got = swap(jnp.concatenate([pieces, same(extra)], axis=1), ROW)
    grad_raw_rows = got[:, :rows].reshape(nrow * rows, wide)
    extra = jnp.sum(got[:, rows:].astype(f32), axis=0).reshape(2, -1).sum(axis=0)

    head = jnp.dot(normed_rows.T, grad_raw_rows, preferred_element_type=f32)
    head = head.reshape(nzh, part_rows, nzl * nc, part_cols).transpose(0, 2, 1, 3)
    head = head.reshape(ncol, part_rows, part_cols).astype(b16)
    high, low = halves(extra.reshape(-1, part_cols))
    side = jnp.concatenate([high, low], axis=0)
    side = jnp.pad(side, ((0, part_rows - side.shape[0]), (0, 0)))
    side = jnp.broadcast_to(side[None], (ncol,) + side.shape)
    got = swap(jnp.concatenate([head, side], axis=2), COL).astype(f32)
    got = jnp.sum(got, axis=0)
    grad_head = got[:, :part_cols]
    side = got[:32, part_cols:].reshape(2, -1).sum(axis=0)
    grad_gain = side[:depth]
    loss = side[depth] / (2.0 * total)

    spread_gain = grad_normed * gain
    inner = jnp.mean(spread_gain * scaled, axis=-1, keepdims=True)
    grad_pooled = (spread_gain - scaled * inner) / radius
    grad_features = jnp.broadcast_to((grad_pooled / window)[:, None, :], features.shape)
    return (loss, grad_features.astype(b16), grad_head, grad_gain)


def solution(mesh):
    fine = Mesh(mesh.devices.reshape(4, 4, 4, 2, 2), AXES)
    whole = P(AXES)
    in_specs = (P(AXES, None, None), P(AXES, None), P(), P(), whole)
    out_specs = (P(), P(AXES, None, None), P(("zh", "y"), ("x", "zl", "c")), P())
    return jax.shard_map(body, mesh=fine, in_specs=in_specs, out_specs=out_specs, check_vma=False)
```

```python
import jax
import jax.numpy as jnp
from jax import lax
from jax.experimental import pallas as pl
from jax.experimental.pallas import tpu as pltpu
from jax.sharding import Mesh, PartitionSpec as P

logit_scale = 64.0
norm_eps = 1e-06

AXES = ("zh", "y", "x", "zl", "c")
ROW = ("y", "x")
COL = ("zh", "zl", "c")

D, E, ROWS = 768, 1024, 32
SIDE = 512
MARK = 128
CHUNK = 128
f32, b16 = jnp.float32, jnp.bfloat16
VMEM = pl.BlockSpec(memory_space=pltpu.VMEM)
SMEM = pl.BlockSpec(memory_space=pltpu.SMEM)


def unit_rows(raw):
    length = jnp.sqrt(jnp.sum(raw * raw, axis=-1, keepdims=True) + norm_eps)
    return (raw / length, length)


def swap(blocks, axes):
    return lax.all_to_all(blocks, axes, 0, 0, tiled=True)


def same(block, peers):
    return jnp.broadcast_to(block[None], (peers,) + block.shape)


def halves(value):
    high = value.astype(b16)
    return high, (value - high.astype(f32)).astype(b16)


def other_core(block):
    return lax.ppermute(block, "c", [(0, 1), (1, 0)])


def along_z(block, step):
    pairs = []
    for z in range(8):
        pairs += [(2 * z, 2 * ((z + step) % 8)), (2 * z + 1, 2 * ((z - step) % 8) + 1)]
    return lax.ppermute(block, COL, pairs)


def gather_columns(block):
    chip = jnp.concatenate([block, other_core(block)], axis=0)
    near = [along_z(chip, 1), along_z(chip, 2), along_z(chip, 3), along_z(block, 4)]
    near = jnp.concatenate(near, axis=0)
    return chip, near, other_core(near)


def wanted_mask(marks, shift):
    marks = marks.astype(f32)
    wanted = marks[:, 0:1] * 128.0 + marks[:, 1:2]
    place = lax.broadcasted_iota(jnp.int32, (1, SIDE), 1)
    ids = (place >> 7) * 2048 + shift * 128 + (place & 127)
    return wanted == ids.astype(f32)


def lanes_to_rows(row):
    return jnp.transpose(jnp.broadcast_to(row, (128, row.shape[1])))


def scores_kernel(where, got, head, chip, near, far, expo, teach, row_part, col_part, pos_part):
    z, c, shift = where[0], where[1], where[2]
    up = 1 - 2 * c

    def put(ref, start, zz, cc):
        slot = pl.multiple_of((((zz + 16) & 7) * 2 + cc) * ROWS, ROWS)
        teach[pl.ds(slot, ROWS), :] = ref[start : start + ROWS, :]

    put(chip, 0, z, c)
    put(chip, ROWS, z, 1 - c)
    for ref, cc, sign in ((near, c, -up), (far, 1 - c, up)):
        for k in (1, 2, 3):
            put(ref, (k - 1) * 2 * ROWS, z + sign * k, cc)
            put(ref, (k - 1) * 2 * ROWS + ROWS, z + sign * k, 1 - cc)
        put(ref, 6 * ROWS, z + 4, cc)

    col = jnp.zeros((1, SIDE), f32)
    pos = jnp.zeros((1, SIDE), f32)
    for n in range(SIDE // CHUNK):
        at = slice(n * CHUNK, (n + 1) * CHUNK)
        raw = jnp.dot(got[at, :D], head[...], preferred_element_type=f32)
        student = unit_rows(raw)[0].astype(b16)
        scores = logit_scale * lax.dot_general(
            student, teach[...], (((1,), (1,)), ((), ())), preferred_element_type=f32
        )
        mask = wanted_mask(got[at, D:], shift)
        pos = pos + jnp.sum(jnp.where(mask, scores, 0.0), axis=0, keepdims=True)
        e = jnp.exp(scores)
        expo[at, :] = e
        col = col + jnp.sum(e, axis=0, keepdims=True)
        lanes = sum(e[:, k : k + 128] for k in range(0, SIDE, 128))
        row_part[:, at] = jnp.sum(jnp.transpose(lanes), axis=0, keepdims=True)
    col_part[...] = col
    pos_part[...] = pos


def weights_kernel(where, got, expo, teach, row_in, col_in, terms, row_sums, col_sums):
    shift = where[2]
    rows = jnp.sum(row_in[...], axis=0)
    cols = jnp.sum(col_in[...], axis=0)
    row_sums[...] = rows
    col_sums[...] = cols
    col_inv = 1.0 / cols
    row_inv = lanes_to_rows(1.0 / rows)
    for n in range(SIDE // CHUNK):
        at = slice(n * CHUNK, (n + 1) * CHUNK)
        mask = wanted_mask(got[at, D:], shift)
        scale = col_inv + jnp.concatenate([row_inv[at, :]] * (SIDE // 128), axis=1)
        weights = expo[at, :] * scale - jnp.where(mask, 2.0, 0.0)
        terms[at, :] = jnp.dot(
            weights.astype(b16), teach[...], preferred_element_type=f32
        ).astype(b16)


def shaped(*shape, dtype=f32):
    return jax.ShapeDtypeStruct(shape, dtype)


def body(features, teacher, gain, w_head, positives):
    rows, width = teacher.shape
    depth, window = features.shape[2], features.shape[1]
    nzh, ny, nx, nzl, nc = (lax.axis_size(a) for a in AXES)
    nrow, ncol = ny * nx, nzh * nzl * nc
    total = rows * nrow * ncol
    part_rows, part_cols = depth // (nzh * ny), width // (nx * nzl * nc)
    zh, y, x, zl, c = (lax.axis_index(a) for a in AXES)
    where = jnp.stack([zh * nzl + zl, c, y * nx + x]).astype(jnp.int32)

    teacher_unit = unit_rows(teacher.astype(f32))[0].astype(b16)
    chip, near, far = gather_columns(teacher_unit)

    pooled = jnp.mean(features, axis=1, dtype=f32)
    radius = jnp.sqrt(jnp.mean(pooled * pooled, axis=-1, keepdims=True) + norm_eps)
    scaled = pooled / radius
    normed = (scaled * gain).astype(b16)
    marks = jnp.stack([positives // 128, positives % 128], axis=1).astype(b16)
    marks = jnp.pad(marks, ((0, 0), (0, MARK - 2)))
    got = swap(same(jnp.concatenate([normed, marks], axis=1), nrow), ROW)
    got = got.reshape(nrow * rows, -1)

    raw = jnp.dot(normed, w_head, preferred_element_type=f32)
    unit, length = unit_rows(raw)

    expo, teach, row_part, col_part, pos_part = pl.pallas_call(
        scores_kernel,
        out_shape=[
            shaped(SIDE, SIDE),
            shaped(SIDE, E, dtype=b16),
            shaped(1, SIDE),
            shaped(1, SIDE),
            shaped(1, SIDE),
        ],
        in_specs=[SMEM] + [VMEM] * 5,
        out_specs=[VMEM] * 5,
        compiler_params=pltpu.CompilerParams(vmem_limit_bytes=32 << 20),
        name="scores",
    )(where, got, w_head, chip, near, far)
    row_in = swap(same(row_part, nrow), ROW)
    col_in = swap(same(col_part, ncol), COL)
    terms, row_sums, col_sums = pl.pallas_call(
        weights_kernel,
        out_shape=[shaped(SIDE, E, dtype=b16), shaped(1, SIDE), shaped(1, SIDE)],
        in_specs=[SMEM] + [VMEM] * 5,
        out_specs=[VMEM] * 3,
        compiler_params=pltpu.CompilerParams(vmem_limit_bytes=32 << 20),
        name="weights",
    )(where, got, expo, teach, row_in, col_in)
    loss_part = (
        jnp.sum(jnp.log(row_sums)) / nrow
        + jnp.sum(jnp.log(col_sums)) / ncol
        - 2.0 * jnp.sum(pos_part)
    )

    terms = swap(terms.reshape(nrow, rows, width), ROW)
    grad_unit = logit_scale * jnp.sum(terms.astype(f32), axis=0)
    along = jnp.sum(unit * grad_unit, axis=-1, keepdims=True)
    grad_raw = ((grad_unit - unit * along) / length).astype(b16)
    grad_normed = jnp.dot(grad_raw, w_head.T, preferred_element_type=f32)
    gain_part = jnp.sum(grad_normed * scaled, axis=0)

    wide = width // nx
    pieces = grad_raw.reshape(rows, nx, wide).transpose(1, 0, 2)
    pieces = jnp.broadcast_to(pieces[None], (ny,) + pieces.shape).reshape(nrow, rows, wide)
    extra = jnp.concatenate([gain_part, loss_part[None], jnp.zeros((255,), f32)])
    extra = jnp.concatenate(halves(extra)).reshape(-1, wide)
    back = swap(jnp.concatenate([pieces, same(extra, nrow)], axis=1), ROW)
    grad_raw_rows = back[:, :rows].reshape(nrow * rows, wide)
    extra = jnp.sum(back[:, rows:].astype(f32), axis=0).reshape(2, -1).sum(axis=0)

    normed_rows = got[:, :D].reshape(nrow * rows, nzh, ny, part_rows)
    normed_rows = lax.dynamic_index_in_dim(normed_rows, y, 2, keepdims=False)
    normed_rows = normed_rows.reshape(nrow * rows, nzh * part_rows)
    head = jnp.dot(normed_rows.T, grad_raw_rows, preferred_element_type=f32)
    head = head.reshape(nzh, part_rows, nzl * nc, part_cols).transpose(0, 2, 1, 3)
    head = head.reshape(ncol, part_rows, part_cols).astype(b16)
    high, low = halves(extra.reshape(-1, part_cols))
    side = jnp.concatenate([high, low], axis=0)
    side = jnp.pad(side, ((0, part_rows - side.shape[0]), (0, 0)))
    last = swap(jnp.concatenate([head, same(side, ncol)], axis=2), COL).astype(f32)
    last = jnp.sum(last, axis=0)
    grad_head = last[:, :part_cols]
    side = last[:32, part_cols:].reshape(2, -1).sum(axis=0)
    grad_gain = side[:depth]
    loss = side[depth] / (2.0 * total)

    spread_gain = grad_normed * gain
    inner = jnp.mean(spread_gain * scaled, axis=-1, keepdims=True)
    grad_pooled = (spread_gain - scaled * inner) / radius
    grad_features = jnp.broadcast_to((grad_pooled / window)[:, None, :], features.shape)
    return (loss, grad_features.astype(b16), grad_head, grad_gain)


def solution(mesh):
    fine = Mesh(mesh.devices.reshape(4, 4, 4, 2, 2), AXES)
    in_specs = (P(AXES, None, None), P(AXES, None), P(), P(), P(AXES))
    out_specs = (P(), P(AXES, None, None), P(("zh", "y"), ("x", "zl", "c")), P())
    return jax.shard_map(body, mesh=fine, in_specs=in_specs, out_specs=out_specs, check_vma=False)
```

```python
import jax
import jax.numpy as jnp
from jax import lax
from jax.experimental import pallas as pl
from jax.experimental.pallas import tpu as pltpu
from jax.sharding import Mesh, PartitionSpec as P

logit_scale = 64.0
norm_eps = 1e-06

AXES = ("zh", "y", "x", "zl", "c")
ROW = ("x", "zl")
CHIPS = ("zh", "y")

D, E, OWN, WIN = 768, 1024, 32, 32
NROW, NCHIP, NCOL = 8, 16, 32
SIDE = NROW * OWN
HALF = NCHIP * OWN
MARK = 128
CHUNK = 128
f32, b16 = jnp.float32, jnp.bfloat16
VMEM = pl.BlockSpec(memory_space=pltpu.VMEM)
SMEM = pl.BlockSpec(memory_space=pltpu.SMEM)
ANY = pl.BlockSpec(memory_space=pl.ANY)
PARAMS = pltpu.CompilerParams(vmem_limit_bytes=32 << 20)


def shaped(*shape, dtype=f32):
    return jax.ShapeDtypeStruct(shape, dtype)


def unit_rows(raw):
    length = jnp.sqrt(jnp.sum(raw * raw, axis=-1, keepdims=True) + norm_eps)
    return (raw / length, length)


def swap(blocks, axes):
    return lax.all_to_all(blocks, axes, 0, 0, tiled=True)


def spread(block, axes):
    peers = lax.axis_size(axes)
    return swap(jnp.broadcast_to(block[None], (peers,) + block.shape), axes)


def other(block, axis):
    return lax.ppermute(block, axis, [(0, 1), (1, 0)])


def along_x(block, step):
    return lax.ppermute(block, "x", [(i, (i + step) % 4) for i in range(4)])


def halves(value):
    high = value.astype(b16)
    return high, (value - high.astype(f32)).astype(b16)


def product(left, right, left_dim, right_dim):
    dims = (((left_dim,), (right_dim,)), ((), ()))
    return lax.dot_general(left, right, dims, preferred_element_type=f32)


def teacher_kernel(teacher, out):
    out[...] = unit_rows(teacher[...].astype(f32))[0].astype(b16)


def student_kernel(where, mine, pair, one, two, three, head, rows, student):
    x, zl = where[0], where[1]

    def put(ref, start, xx, zz):
        slot = pl.multiple_of((((xx + 4) & 3) * 2 + zz) * OWN, OWN)
        rows[pl.ds(slot, OWN), :] = ref[start : start + OWN, :]

    put(mine, 0, x, zl)
    put(pair, 0, x, 1 - zl)
    for k, ref in ((1, one), (2, two), (3, three)):
        put(ref, 0, x - k, zl)
        put(ref, OWN, x - k, 1 - zl)
    for n in range(SIDE // CHUNK):
        at = slice(n * CHUNK, (n + 1) * CHUNK)
        raw = jnp.dot(rows[at, :D], head[...], preferred_element_type=f32)
        student[at, :] = unit_rows(raw)[0].astype(b16)


def wanted_mask(marks, where, core):
    marks = marks.astype(f32)
    wanted = marks[:, 0:1] * 128.0 + marks[:, 1:2]
    place = lax.broadcasted_iota(jnp.int32, (1, HALF), 1)
    ids = (place >> 7) * 512 + ((place >> 5) & 3) * 2048 + (place & 31)
    ids = ids + where[0] * 128 + where[1] * 64 + core * 32
    return wanted == ids.astype(f32)


def scores_kernel(where, student, rows, mine, pair, expo, row_part, col_part, pos_part):
    core = where[2]
    for part, (ref, cc) in enumerate(((mine, core), (pair, 1 - core))):
        col = jnp.zeros((1, HALF), f32)
        pos = jnp.zeros((1, HALF), f32)
        for n in range(SIDE // CHUNK):
            at = slice(n * CHUNK, (n + 1) * CHUNK)
            scores = logit_scale * product(student[at, :], ref[...], 1, 1)
            mask = wanted_mask(rows[at, D:], where, cc)
            pos = pos + jnp.sum(jnp.where(mask, scores, 0.0), axis=0, keepdims=True)
            e = jnp.exp(scores)
            expo[at, part * HALF : (part + 1) * HALF] = e
            col = col + jnp.sum(e, axis=0, keepdims=True)
            lanes = sum(e[:, k : k + 128] for k in range(0, HALF, 128))
            if part == 0:
                row_part[at, :] = lanes
            else:
                row_part[at, :] += lanes
        col_part[:, pl.ds(pl.multiple_of(cc * HALF, HALF), HALF)] = col
        pos_part[:, part * HALF : (part + 1) * HALF] = pos


def plain_kernel(expo, row_part, mine, pair, terms):
    for n in range(SIDE // CHUNK):
        at = slice(n * CHUNK, (n + 1) * CHUNK)
        left = expo[at, :].astype(b16)
        out = product(left[:, :HALF], mine[...], 1, 0) + product(left[:, HALF:], pair[...], 1, 0)
        terms[at, :E] = out.astype(b16)
        high, low = halves(jnp.sum(row_part[at, :], axis=1, keepdims=True))
        lane = lax.broadcasted_iota(jnp.int32, (CHUNK, MARK), 1)
        high, low = high.astype(f32), low.astype(f32)
        terms[at, 2 * E :] = jnp.where(lane < 64, high, low).astype(b16)


def scaled_kernel(where, rows, expo, mine, pair, col_in, pos_part, _, terms, tail, sums):
    core = where[2]
    cols = jnp.sum(col_in[...], axis=0)
    sums[...] = cols
    tail[...] = jnp.log(cols) * (1.0 / NCOL) - 2.0 * pos_part[...]
    for n in range(SIDE // CHUNK):
        at = slice(n * CHUNK, (n + 1) * CHUNK)
        out = jnp.zeros((CHUNK, E), f32)
        for part, (ref, cc) in enumerate(((mine, core), (pair, 1 - core))):
            inv = 1.0 / sums[:, pl.ds(pl.multiple_of(cc * HALF, HALF), HALF)]
            mask = wanted_mask(rows[at, D:], where, cc)
            e = expo[at, part * HALF : (part + 1) * HALF]
            weights = (e * inv - jnp.where(mask, 2.0, 0.0)).astype(b16)
            out = out + product(weights, ref[...], 1, 0)
        terms[at, E : 2 * E] = out.astype(b16)


def rows_kernel(terms, unit, length, scaled, radius, gain, head, tail, sent, pooled_grad):
    plain = jnp.zeros((OWN, E), f32)
    weighted = jnp.zeros((OWN, E), f32)
    sums = jnp.zeros((OWN, MARK), f32)
    for s in range(NROW):
        plain = plain + terms[s, :, :E].astype(f32)
        weighted = weighted + terms[s, :, E : 2 * E].astype(f32)
        sums = sums + terms[s, :, 2 * E :].astype(f32)
    row_sums = sums[:, 0:1] + sums[:, 64:65]
    unit_ = unit[...]
    grad_unit = logit_scale * (plain / row_sums + weighted)
    along = jnp.sum(unit_ * grad_unit, axis=-1, keepdims=True)
    grad_raw = ((grad_unit - unit_ * along) / length[...]).astype(b16)
    grad_normed = product(grad_raw, head[...], 1, 1)
    scaled_ = scaled[...]
    gain_part = jnp.sum(grad_normed * scaled_, axis=0, keepdims=True)
    loss = jnp.sum(jnp.log(row_sums), axis=0, keepdims=True)
    loss = loss + jnp.sum(tail[...], axis=1, keepdims=True)
    pieces = [gain_part[:, k * 128 : (k + 1) * 128] for k in range(D // 128)]
    pieces += [jnp.broadcast_to(loss, (1, 128)), jnp.zeros((1, 128), f32)]
    extra = jnp.concatenate(halves(jnp.concatenate(pieces, axis=0)), axis=0)
    for s in range(NROW):
        sent[s, :OWN, :] = grad_raw[:, s * 128 : (s + 1) * 128]
        sent[s, OWN:, :] = extra
    spread_gain = grad_normed * gain[...]
    inner = jnp.mean(spread_gain * scaled_, axis=-1, keepdims=True)
    grad = (spread_gain - scaled_ * inner) / radius[...]
    pooled_grad[...] = (grad / WIN).astype(b16)


def head_kernel(back, rows, sent):
    grad_raw = back[:, :OWN, :].reshape(SIDE, 128)
    head = product(rows[:, :D], grad_raw, 0, 0).astype(b16)
    extra = jnp.sum(back[:, OWN : OWN + 8, :].astype(f32), axis=0)
    extra = extra + jnp.sum(back[:, OWN + 8 :, :].astype(f32), axis=0)
    extra = jnp.concatenate(halves(extra), axis=0)
    for g in range(NCHIP):
        sent[g, :48, :] = head[g * 48 : (g + 1) * 48, :]
        sent[g, 48:, :] = extra


def last_kernel(back, _, out):
    total = jnp.sum(back[...].astype(f32), axis=0)
    out[:48, :] = total[:48]
    out[48:, :] = total[48:56] + total[56:]


def call(kernel, out, n_in, name, where=False, specs=None, **options):
    specs = specs or ([SMEM] if where else []) + [VMEM] * n_in
    return pl.pallas_call(
        kernel,
        out_shape=out,
        in_specs=specs,
        out_specs=[VMEM] * len(out) if isinstance(out, list) else VMEM,
        compiler_params=PARAMS,
        name=name,
        **options,
    )


def body(features, teacher, gain, w_head, positives):
    x, zl, c = (lax.axis_index(a) for a in ("x", "zl", "c"))
    where = jnp.stack([x, zl, c]).astype(jnp.int32)
    total = OWN * NROW * NCOL

    mine = call(teacher_kernel, shaped(OWN, E, dtype=b16), 1, "teacher")(teacher)
    mine = spread(mine, "zh").reshape(4 * OWN, E)
    mine = spread(mine, "y").reshape(HALF, E)
    pair = other(mine, "c")

    pooled = jnp.mean(features, axis=1, dtype=f32)
    radius = jnp.sqrt(jnp.mean(pooled * pooled, axis=-1, keepdims=True) + norm_eps)
    scaled = pooled / radius
    normed = (scaled * gain).astype(b16)
    marks = jnp.stack([positives // 128, positives % 128], axis=1).astype(b16)
    own = jnp.concatenate([normed, jnp.pad(marks, ((0, 0), (0, MARK - 2)))], axis=1)
    near = other(own, "zl")
    both = jnp.concatenate([own, near], axis=0)
    rows, student = call(
        student_kernel,
        [shaped(SIDE, D + MARK, dtype=b16), shaped(SIDE, E, dtype=b16)],
        6,
        "student",
        True,
    )(where, own, near, along_x(both, 1), along_x(both, 2), along_x(both, 3), w_head)
    raw = jnp.dot(normed, w_head, preferred_element_type=f32)
    unit, length = unit_rows(raw)

    expo, row_part, col_part, pos_part = call(
        scores_kernel,
        [shaped(SIDE, 2 * HALF), shaped(SIDE, 128), shaped(1, 2 * HALF), shaped(1, 2 * HALF)],
        4,
        "scores",
        True,
    )(where, student, rows, mine, pair)
    col_in = spread(col_part + other(col_part, "c"), CHIPS)
    message = shaped(SIDE, 2 * E + MARK, dtype=b16)
    terms = call(plain_kernel, message, 4, "plain")(expo, row_part, mine, pair)
    terms, tail, _ = call(
        scaled_kernel,
        [message, shaped(1, 2 * HALF), shaped(1, 2 * HALF)],
        7,
        "scaled",
        True,
        input_output_aliases={7: 0},
    )(where, rows, expo, mine, pair, col_in, pos_part, terms)

    terms = swap(terms.reshape(NROW, OWN, 2 * E + MARK), ROW)
    sent, pooled_grad = call(
        rows_kernel, [shaped(NROW, 48, 128, dtype=b16), shaped(OWN, D, dtype=b16)], 8, "rows"
    )(terms, unit, length, scaled, radius, gain[None], w_head, tail)
    grad_features = jnp.broadcast_to(pooled_grad[:, None, :], features.shape)

    back = swap(sent, ROW)
    sent = call(head_kernel, shaped(NCHIP, 64, 128, dtype=b16), 2, "head")(back, rows)
    back = swap(sent, CHIPS)
    last = call(last_kernel, shaped(56, 128), 2, "last", specs=[VMEM, ANY])(back, grad_features)
    last = last + other(last, "c")
    grad_head = lax.dynamic_slice(last, (0, c * 64), (48, 64))
    return (last[54, 0] / (2.0 * total), grad_features, grad_head, last[48:54].reshape(D))


def solution(mesh):
    fine = Mesh(mesh.devices.reshape(4, 4, 4, 2, 2), AXES)
    in_specs = (P(AXES, None, None), P(AXES, None), P(), P(), P(AXES))
    out_specs = (P(), P(AXES, None, None), P(("zh", "y"), ("x", "zl", "c")), P())
    return jax.shard_map(body, mesh=fine, in_specs=in_specs, out_specs=out_specs, check_vma=False)
```

```python
import jax
import jax.numpy as jnp
from jax import lax
from jax.experimental import pallas as pl
from jax.experimental.pallas import tpu as pltpu
from jax.sharding import Mesh, PartitionSpec as P

logit_scale = 64.0
norm_eps = 1e-06

AXES = ("zh", "y", "x", "zl", "c")
ROW = ("x", "zl")
CHIPS = ("zh", "y")

D, E, OWN, WIN = 768, 1024, 32, 32
NROW, NCHIP, NCOL = 8, 16, 32
SIDE = NROW * OWN
HALF = NCHIP * OWN
MARK = 128
CHUNK = 128
BLOCK = 4 * OWN
f32, b16 = jnp.float32, jnp.bfloat16
SPACES = {
    "V": pl.BlockSpec(memory_space=pltpu.VMEM),
    "S": pl.BlockSpec(memory_space=pltpu.SMEM),
    "H": pl.BlockSpec(memory_space=pltpu.HBM),
    "A": pl.BlockSpec(memory_space=pl.ANY),
}
SMALL, SCORES = 12 << 20, 12 << 20


def shaped(*shape, dtype=f32):
    return jax.ShapeDtypeStruct(shape, dtype)


def unit_rows(raw):
    length = jnp.sqrt(jnp.sum(raw * raw, axis=-1, keepdims=True) + norm_eps)
    return (raw / length, length)


def swap(blocks, axes):
    return lax.all_to_all(blocks, axes, 0, 0, tiled=True)


def spread(block, axes):
    peers = lax.axis_size(axes)
    return swap(jnp.broadcast_to(block[None], (peers,) + block.shape), axes)


def other(block, axis):
    return lax.ppermute(block, axis, [(0, 1), (1, 0)])


def along(block, axis, step):
    return lax.ppermute(block, axis, [(i, (i + step) % 4) for i in range(4)])


def halves(value):
    high = value.astype(b16)
    return high, (value - high.astype(f32)).astype(b16)


def product(left, right, left_dim, right_dim):
    dims = (((left_dim,), (right_dim,)), ((), ()))
    return lax.dot_general(left, right, dims, preferred_element_type=f32)


def teacher_kernel(teacher, out):
    out[...] = unit_rows(teacher[...].astype(f32))[0].astype(b16)


def flat(gain):
    return jnp.concatenate([gain[k : k + 1, :] for k in range(D // 128)], axis=1)


def norm_kernel(features, places, gain, sent, scaled, radius):
    for n in range(0, OWN, 8):
        at = slice(n, n + 8)
        pooled = jnp.sum(features[at].astype(f32), axis=1) * (1.0 / WIN)
        size = jnp.sqrt(jnp.mean(pooled * pooled, axis=-1, keepdims=True) + norm_eps)
        radius[at, :] = size
        scaled[at, :] = pooled / size
    value = (scaled[...] * flat(gain)).astype(b16)
    place = places[...]
    lane = lax.broadcasted_iota(jnp.int32, place.shape, 1)
    marks = jnp.where(lane == 0, place >> 7, place & 127).astype(f32).astype(b16)
    for s in range(NROW):
        sent[s, :, :D] = value
        sent[s, :, D:] = marks


def position():
    return [lax.axis_index(a) for a in ("y", "x", "zl", "c", "zh")]


def student_kernel(rows, head, student, unit, length, full, sizes):
    raw = jnp.dot(rows[:, :D], head[...], preferred_element_type=f32)
    full[...], sizes[...] = unit_rows(raw)
    student[...] = full[...].astype(b16)
    where = position()
    own = pl.ds(pl.multiple_of((where[1] * 2 + where[2]) * OWN, OWN), OWN)
    unit[...] = full[own, :]
    length[...] = sizes[own, :]


def place(where, k):
    core = where[3] if k % 2 == 0 else 1 - where[3]
    y = (where[0] + (0, 3, 1, 2)[k // 2]) & 3
    return core, y


def wanted_mask(marks, where, k):
    core, y = place(where, k)
    marks = marks.astype(f32)
    wanted = marks[:, 0:1] * 128.0 + marks[:, 1:2]
    lane = lax.broadcasted_iota(jnp.int32, (1, BLOCK), 1)
    ids = (lane >> 5) * 2048 + (lane & 31) + y * 512 + where[1] * 128 + where[2] * 64 + core * 32
    return wanted == ids.astype(f32)


def fetch(where, sides, teach, sems):
    copies = []
    for k in range(8):
        for n in range(4):
            slot = pl.multiple_of(((where[4] + 4 - n) & 3) * OWN, OWN)
            here = sides[k % 2].at[pl.ds(k // 2 * BLOCK + n * OWN, OWN), :]
            there = teach.at[pl.ds(k * BLOCK + slot, OWN), :]
            copies.append(pltpu.make_async_copy(here, there, sems.at[4 * k + n]))
            copies[-1].start()
    return copies


def scores_kernel(student, rows, near, pair, teach, expo, terms, col_part, pos_part, sems):
    where = position()
    copies = fetch(where, (near, pair), teach, sems)
    lanes = [jnp.zeros((CHUNK, 128), f32) for _ in range(SIDE // CHUNK)]
    pos = jnp.zeros((1, BLOCK), f32)
    for k in range(0, 8, 2):
        for copy in copies[4 * k : 4 * k + 8]:
            copy.wait()
        both = product(student[...], teach[k * BLOCK : (k + 2) * BLOCK, :], 1, 1)
        for j in (k, k + 1):
            col = jnp.zeros((1, BLOCK), f32)
            for n in range(SIDE // CHUNK):
                at = slice(n * CHUNK, (n + 1) * CHUNK)
                value = logit_scale * both[at, (j - k) * BLOCK : (j - k + 1) * BLOCK]
                mask = wanted_mask(rows[at, D:], where, j)
                pos = pos + jnp.sum(jnp.where(mask, value, 0.0), axis=0, keepdims=True)
                e = jnp.exp(value)
                expo[at, j * BLOCK : (j + 1) * BLOCK] = e.astype(b16)
                col = col + jnp.sum(e, axis=0, keepdims=True)
                lanes[n] = lanes[n] + e
            core, y = place(where, j)
            col_part[pl.ds(core * 4 + y, 1), :] = col
    pos_part[...] = pos
    for n in range(SIDE // CHUNK):
        at = slice(n * CHUNK, (n + 1) * CHUNK)
        high, low = halves(jnp.sum(lanes[n], axis=1, keepdims=True))
        lane = lax.broadcasted_iota(jnp.int32, (CHUNK, MARK), 1)
        terms[at, E : E + MARK] = jnp.where(lane < 64, high.astype(f32), low.astype(f32)).astype(b16)
    terms[:, :E] = product(expo[...], teach[...], 1, 0).astype(b16)


def cols_kernel(mine, pair, sent):
    total = mine[...] + pair[...]
    for g in range(NCHIP):
        sent[g] = total


def scaled_kernel(rows, col_in, pos_part, expo, teach, _, terms, tail, weights, inv):
    where = position()
    cols = jnp.sum(col_in[...], axis=0)
    logs = jnp.sum(jnp.log(cols), axis=0, keepdims=True)
    tail[...] = logs * (1.0 / NCOL) - 2.0 * pos_part[...]
    inv[...] = 1.0 / cols
    for k in range(8):
        core, y = place(where, k)
        scale = inv[pl.ds(core * 4 + y, 1), :]
        at = slice(k * BLOCK, (k + 1) * BLOCK)
        mask = wanted_mask(rows[:, D:], where, k)
        value = expo[:, at].astype(f32) * scale - jnp.where(mask, 2.0, 0.0)
        weights[:, at] = value.astype(b16)
    terms[:, E + MARK :] = product(weights[...], teach[...], 1, 0).astype(b16)


def rows_kernel(terms, unit, length, scaled, radius, gain, head, tail, sent, pooled_grad):
    plain = jnp.zeros((OWN, E), f32)
    weighted = jnp.zeros((OWN, E), f32)
    sums = jnp.zeros((OWN, MARK), f32)
    for s in range(NROW):
        plain = plain + terms[s, :, :E].astype(f32)
        sums = sums + terms[s, :, E : E + MARK].astype(f32)
        weighted = weighted + terms[s, :, E + MARK :].astype(f32)
    row_sums = sums[:, 0:1] + sums[:, 64:65]
    unit_ = unit[...]
    grad_unit = logit_scale * (plain / row_sums + weighted)
    along = jnp.sum(unit_ * grad_unit, axis=-1, keepdims=True)
    grad_raw = ((grad_unit - unit_ * along) / length[...]).astype(b16)
    grad_normed = product(grad_raw, head[...], 1, 1)
    scaled_ = scaled[...]
    gain_part = jnp.sum(grad_normed * scaled_, axis=0, keepdims=True)
    loss = jnp.sum(jnp.log(row_sums), axis=0, keepdims=True)
    loss = loss + jnp.sum(tail[...], axis=1, keepdims=True)
    pieces = [gain_part[:, k * 128 : (k + 1) * 128] for k in range(D // 128)]
    pieces += [jnp.broadcast_to(loss, (1, 128)), jnp.zeros((1, 128), f32)]
    extra = jnp.concatenate(halves(jnp.concatenate(pieces, axis=0)), axis=0)
    for s in range(NROW):
        sent[s, :OWN, :] = grad_raw[:, s * 128 : (s + 1) * 128]
        sent[s, OWN:, :] = extra
    spread_gain = grad_normed * flat(gain)
    inner = jnp.mean(spread_gain * scaled_, axis=-1, keepdims=True)
    grad = (spread_gain - scaled_ * inner) / radius[...]
    pooled_grad[...] = (grad / WIN).astype(b16)


def head_kernel(back, rows, sent):
    grad_raw = back[:, :OWN, :].reshape(SIDE, 128)
    head = product(rows[:, :D], grad_raw, 0, 0).astype(b16)
    extra = jnp.sum(back[:, OWN : OWN + 8, :].astype(f32), axis=0)
    extra = extra + jnp.sum(back[:, OWN + 8 :, :].astype(f32), axis=0)
    extra = jnp.concatenate(halves(extra), axis=0)
    for g in range(NCHIP):
        sent[g, :48, :] = head[g * 48 : (g + 1) * 48, :]
        sent[g, 48:, :] = extra


def last_kernel(back, _, out):
    total = jnp.sum(back[...].astype(f32), axis=0)
    out[:48, :] = total[:48]
    out[48:, :] = total[48:56] + total[56:]


def out_kernel(mine, pair, head, gain, loss):
    total = mine[...] + pair[...]
    head[...] = jnp.where(position()[3] == 0, total[:48, :64], total[:48, 64:])
    gain[...] = total[48 : 48 + D // 128, :]
    loss[...] = total[54:55, :] * (1.0 / (2.0 * OWN * NROW * NCOL))


def call(kernel, out, ins, name, outs=None, limit=SMALL, **options):
    out_specs = [SPACES[k] for k in outs or "V" * (len(out) if isinstance(out, list) else 1)]
    return pl.pallas_call(
        kernel,
        out_shape=out,
        in_specs=[SPACES[k] for k in ins],
        out_specs=out_specs if isinstance(out, list) else out_specs[0],
        compiler_params=pltpu.CompilerParams(vmem_limit_bytes=limit),
        name=name,
        **options,
    )


def body(features, teacher, gain, w_head, positives):
    wide = 2 * HALF

    mine = call(teacher_kernel, shaped(OWN, E, dtype=b16), "V", "teacher")(teacher)
    mine = jnp.concatenate([mine] + [along(mine, "zh", k) for k in (1, 2, 3)], axis=0)

    places = jnp.broadcast_to(positives[:, None], (OWN, MARK))
    gain = gain.reshape(D // 128, 128)
    own, scaled, radius = call(
        norm_kernel,
        [
            shaped(NROW, OWN, D + MARK, dtype=b16),
            shaped(OWN, D),
            shaped(OWN, 1),
        ],
        "VVV",
        "norm",
    )(features, places, gain)

    mine, own = lax.optimization_barrier((mine, own))
    up, down = along(mine, "y", 1), along(mine, "y", 3)
    far = along(up, "y", 1)
    rows = swap(own, ROW).reshape(SIDE, D + MARK)
    student, unit, length = call(
        student_kernel,
        [shaped(SIDE, E, dtype=b16), shaped(OWN, E), shaped(OWN, 1)],
        "VV",
        "student",
        scratch_shapes=[pltpu.VMEM((SIDE, E), f32), pltpu.VMEM((SIDE, 1), f32)],
    )(rows, w_head)
    far, student = lax.optimization_barrier((far, student))
    near = jnp.concatenate([mine, up, down, far], axis=0)
    pair = other(near, "c")

    message = shaped(SIDE, 2 * E + MARK, dtype=b16)
    teach, expo, terms, col_part, pos_part = call(
        scores_kernel,
        [shaped(wide, E, dtype=b16), shaped(SIDE, wide, dtype=b16), message]
        + [shaped(8, 128), shaped(1, 128)],
        "VVAA",
        "scores",
        limit=SCORES,
        scratch_shapes=[pltpu.SemaphoreType.DMA((32,))],
    )(student, rows, near, pair)
    col_in = call(cols_kernel, shaped(NCHIP, 8, 128), "VV", "cols")(col_part, other(col_part, "c"))
    col_in = swap(col_in, CHIPS)
    terms, tail = call(
        scaled_kernel,
        [message, shaped(1, 128)],
        "VVVVVV",
        "scaled",
        input_output_aliases={5: 0},
        scratch_shapes=[pltpu.VMEM((SIDE, wide), b16), pltpu.VMEM((8, 128), f32)],
    )(rows, col_in, pos_part, expo, teach, terms)

    terms = swap(terms.reshape(NROW, OWN, 2 * E + MARK), ROW)
    sent, pooled_grad = call(
        rows_kernel,
        [shaped(NROW, 48, 128, dtype=b16), shaped(OWN, D, dtype=b16)],
        "V" * 8,
        "rows",
    )(terms, unit, length, scaled, radius, gain, w_head, tail)
    grad_features = jnp.broadcast_to(pooled_grad[:, None, :], features.shape)

    back = swap(sent, ROW)
    sent = call(head_kernel, shaped(NCHIP, 64, 128, dtype=b16), "VV", "head")(back, rows)
    back = swap(sent, CHIPS)
    last = call(last_kernel, shaped(56, 128), "VA", "last")(back, grad_features)
    grad_head, grad_gain, loss = call(
        out_kernel, [shaped(48, 64), shaped(D // 128, 128), shaped(1, 128)], "VV", "out"
    )(last, other(last, "c"))
    return (loss[0, 0], grad_features, grad_head, grad_gain.reshape(D))


def solution(mesh):
    fine = Mesh(mesh.devices.reshape(4, 4, 4, 2, 2), AXES)
    in_specs = (P(AXES, None, None), P(AXES, None), P(), P(), P(AXES))
    out_specs = (P(), P(AXES, None, None), P(("zh", "y"), ("x", "zl", "c")), P())
    return jax.shard_map(body, mesh=fine, in_specs=in_specs, out_specs=out_specs, check_vma=False)
```

```python
import jax
import jax.numpy as jnp
from jax import lax
from jax.experimental import pallas as pl
from jax.experimental.pallas import tpu as pltpu
from jax.sharding import Mesh, PartitionSpec as P

logit_scale = 64.0
norm_eps = 1e-06

AXES = ("zh", "y", "x", "zl", "c")
ROW = ("x", "zl")
CHIPS = ("zh", "y")

D, E, OWN, WIN = 768, 1024, 32, 32
NROW, NCHIP, NCOL = 8, 16, 32
SIDE = NROW * OWN
HALF = NCHIP * OWN
MARK = 128
CHUNK = 128
BLOCK = 4 * OWN
f32, b16 = jnp.float32, jnp.bfloat16
SPACES = {
    "V": pl.BlockSpec(memory_space=pltpu.VMEM),
    "S": pl.BlockSpec(memory_space=pltpu.SMEM),
    "H": pl.BlockSpec(memory_space=pltpu.HBM),
    "A": pl.BlockSpec(memory_space=pl.ANY),
}
LIMIT = 12 << 20


def shaped(*shape, dtype=f32):
    return jax.ShapeDtypeStruct(shape, dtype)


def unit_rows(raw):
    length = jnp.sqrt(jnp.sum(raw * raw, axis=-1, keepdims=True) + norm_eps)
    return (raw / length, length)


def swap(blocks, axes):
    return lax.all_to_all(blocks, axes, 0, 0, tiled=True)


def spread(block, axes):
    peers = lax.axis_size(axes)
    return swap(jnp.broadcast_to(block[None], (peers,) + block.shape), axes)


def other(block, axis):
    return lax.ppermute(block, axis, [(0, 1), (1, 0)])


def along(block, axis, step):
    return lax.ppermute(block, axis, [(i, (i + step) % 4) for i in range(4)])


def across(block, flip):
    return lax.ppermute(block, "x", [(i, i ^ flip) for i in range(4)])


def halves(value):
    high = value.astype(b16)
    return high, (value - high.astype(f32)).astype(b16)


def product(left, right, left_dim, right_dim):
    dims = (((left_dim,), (right_dim,)), ((), ()))
    return lax.dot_general(left, right, dims, preferred_element_type=f32)


def teacher_kernel(teacher, out):
    out[...] = unit_rows(teacher[...].astype(f32))[0].astype(b16)


def flat(gain):
    return jnp.concatenate([gain[k : k + 1, :] for k in range(D // 128)], axis=1)


def norm_kernel(features, places, gain, own, scaled, radius):
    for n in range(0, OWN, 8):
        at = slice(n, n + 8)
        pooled = jnp.sum(features[at].astype(f32), axis=1) * (1.0 / WIN)
        size = jnp.sqrt(jnp.mean(pooled * pooled, axis=-1, keepdims=True) + norm_eps)
        radius[at, :] = size
        scaled[at, :] = pooled / size
    value = (scaled[...] * flat(gain)).astype(b16)
    place = places[...]
    lane = lax.broadcasted_iota(jnp.int32, place.shape, 1)
    marks = jnp.where(lane == 0, place >> 7, place & 127).astype(f32).astype(b16)
    own[:, :D] = value
    own[:, D:] = marks


def position():
    return [lax.axis_index(a) for a in ("y", "x", "zl", "c", "zh")]


def student_kernel(four, rest, head, rows, student, unit, length, full, sizes):
    where = position()
    x, zl = where[1], where[2]

    def slot(x_, zl_):
        return pl.ds(pl.multiple_of((((x_ + 4) & 3) * 2 + zl_) * OWN, OWN), OWN)

    for k, (ref, start) in enumerate(((four, 0), (four, 64), (rest, 64), (rest, 0))):
        rows[slot(x ^ k, zl), :] = ref[start : start + OWN, :]
        rows[slot(x ^ k, 1 - zl), :] = ref[start + OWN : start + 2 * OWN, :]
    raw = jnp.dot(rows[:, :D], head[...], preferred_element_type=f32)
    full[...], sizes[...] = unit_rows(raw)
    student[...] = full[...].astype(b16)
    unit[...] = full[slot(x, zl), :]
    length[...] = sizes[slot(x, zl), :]


def place(where, k):
    core = where[3] if k < 4 else 1 - where[3]
    y = (where[0] + (0, 3, 1, 2)[k % 4]) & 3
    return core, y


def wanted_mask(marks, where, k):
    core, y = place(where, k)
    marks = marks.astype(f32)
    wanted = marks[:, 0:1] * 128.0 + marks[:, 1:2]
    lane = lax.broadcasted_iota(jnp.int32, (1, BLOCK), 1)
    ids = (((lane >> 5) + where[4]) & 3) * 2048 + (lane & 31)
    ids = ids + y * 512 + where[1] * 128 + where[2] * 64 + core * 32
    return wanted == ids.astype(f32)


def scores_kernel(student, rows, *refs):
    blocks, (teach, expo, terms, col_part, pos_part) = refs[:8], refs[8:]
    where = position()
    for k, block in enumerate(blocks):
        teach[k * BLOCK : (k + 1) * BLOCK, :] = block[...]
    lanes = [jnp.zeros((CHUNK, 128), f32) for _ in range(SIDE // CHUNK)]
    pos = jnp.zeros((1, BLOCK), f32)
    for k in range(0, 8, 2):
        both = product(student[...], teach[k * BLOCK : (k + 2) * BLOCK, :], 1, 1)
        for j in (k, k + 1):
            col = jnp.zeros((1, BLOCK), f32)
            for n in range(SIDE // CHUNK):
                at = slice(n * CHUNK, (n + 1) * CHUNK)
                value = logit_scale * both[at, (j - k) * BLOCK : (j - k + 1) * BLOCK]
                mask = wanted_mask(rows[at, D:], where, j)
                pos = pos + jnp.sum(jnp.where(mask, value, 0.0), axis=0, keepdims=True)
                e = jnp.exp(value)
                expo[at, j * BLOCK : (j + 1) * BLOCK] = e.astype(b16)
                col = col + jnp.sum(e, axis=0, keepdims=True)
                lanes[n] = lanes[n] + e
            core, y = place(where, j)
            col_part[pl.ds(core * 4 + y, 1), :] = col
    col_part[...] = pltpu.roll(col_part[...], where[4] * OWN, 1)
    pos_part[...] = pos
    for n in range(SIDE // CHUNK):
        at = slice(n * CHUNK, (n + 1) * CHUNK)
        high, low = halves(jnp.sum(lanes[n], axis=1, keepdims=True))
        lane = lax.broadcasted_iota(jnp.int32, (CHUNK, MARK), 1)
        terms[at, E : E + MARK] = jnp.where(lane < 64, high.astype(f32), low.astype(f32)).astype(b16)
    terms[:, :E] = product(expo[...], teach[...], 1, 0).astype(b16)


def cols_kernel(mine, pair, sent):
    total = mine[...] + pair[...]
    for g in range(NCHIP):
        sent[g] = total


def scaled_kernel(rows, col_in, pos_part, expo, teach, _, terms, tail, weights, inv):
    where = position()
    cols = jnp.sum(col_in[...], axis=0)
    logs = jnp.sum(jnp.log(cols), axis=0, keepdims=True)
    tail[...] = logs * (1.0 / NCOL) - 2.0 * pos_part[...]
    inv[...] = pltpu.roll(1.0 / cols, ((4 - where[4]) & 3) * OWN, 1)
    for k in range(8):
        core, y = place(where, k)
        scale = inv[pl.ds(core * 4 + y, 1), :]
        at = slice(k * BLOCK, (k + 1) * BLOCK)
        mask = wanted_mask(rows[:, D:], where, k)
        value = expo[:, at].astype(f32) * scale - jnp.where(mask, 2.0, 0.0)
        weights[:, at] = value.astype(b16)
    terms[:, E + MARK :] = product(weights[...], teach[...], 1, 0).astype(b16)


def rows_kernel(terms, unit, length, scaled, radius, gain, head, tail, sent, pooled_grad):
    plain = jnp.zeros((OWN, E), f32)
    weighted = jnp.zeros((OWN, E), f32)
    sums = jnp.zeros((OWN, MARK), f32)
    for s in range(NROW):
        plain = plain + terms[s, :, :E].astype(f32)
        sums = sums + terms[s, :, E : E + MARK].astype(f32)
        weighted = weighted + terms[s, :, E + MARK :].astype(f32)
    row_sums = sums[:, 0:1] + sums[:, 64:65]
    unit_ = unit[...]
    grad_unit = logit_scale * (plain / row_sums + weighted)
    along = jnp.sum(unit_ * grad_unit, axis=-1, keepdims=True)
    grad_raw = ((grad_unit - unit_ * along) / length[...]).astype(b16)
    grad_normed = product(grad_raw, head[...], 1, 1)
    scaled_ = scaled[...]
    gain_part = jnp.sum(grad_normed * scaled_, axis=0, keepdims=True)
    loss = jnp.sum(jnp.log(row_sums), axis=0, keepdims=True)
    loss = loss + jnp.sum(tail[...], axis=1, keepdims=True)
    pieces = [gain_part[:, k * 128 : (k + 1) * 128] for k in range(D // 128)]
    pieces += [jnp.broadcast_to(loss, (1, 128)), jnp.zeros((1, 128), f32)]
    extra = jnp.concatenate(halves(jnp.concatenate(pieces, axis=0)), axis=0)
    for s in range(NROW):
        sent[s, :OWN, :] = grad_raw[:, s * 128 : (s + 1) * 128]
        sent[s, OWN:, :] = extra
    spread_gain = grad_normed * flat(gain)
    inner = jnp.mean(spread_gain * scaled_, axis=-1, keepdims=True)
    grad = (spread_gain - scaled_ * inner) / radius[...]
    pooled_grad[...] = (grad / WIN).astype(b16)


def head_kernel(back, rows, sent):
    grad_raw = back[:, :OWN, :].reshape(SIDE, 128)
    head = product(rows[:, :D], grad_raw, 0, 0).astype(b16)
    extra = jnp.sum(back[:, OWN : OWN + 8, :].astype(f32), axis=0)
    extra = extra + jnp.sum(back[:, OWN + 8 :, :].astype(f32), axis=0)
    extra = jnp.concatenate(halves(extra), axis=0)
    for g in range(NCHIP):
        sent[g, :48, :] = head[g * 48 : (g + 1) * 48, :]
        sent[g, 48:, :] = extra


def last_kernel(back, _, out):
    total = jnp.sum(back[...].astype(f32), axis=0)
    out[:48, :] = total[:48]
    out[48:, :] = total[48:56] + total[56:]


def out_kernel(mine, pair, head, gain, loss):
    total = mine[...] + pair[...]
    head[...] = jnp.where(position()[3] == 0, total[:48, :64], total[:48, 64:])
    gain[...] = total[48 : 48 + D // 128, :]
    loss[...] = total[54:55, :] * (1.0 / (2.0 * OWN * NROW * NCOL))


def call(kernel, out, ins, name, outs=None, **options):
    out_specs = [SPACES[k] for k in outs or "V" * (len(out) if isinstance(out, list) else 1)]
    return pl.pallas_call(
        kernel,
        out_shape=out,
        in_specs=[SPACES[k] for k in ins],
        out_specs=out_specs if isinstance(out, list) else out_specs[0],
        compiler_params=pltpu.CompilerParams(vmem_limit_bytes=LIMIT),
        name=name,
        **options,
    )


def body(features, teacher, gain, w_head, positives):
    wide = 2 * HALF

    mine = call(teacher_kernel, shaped(OWN, E, dtype=b16), "V", "teacher")(teacher)
    mine = jnp.concatenate([mine] + [along(mine, "zh", k) for k in (3, 2, 1)], axis=0)

    places = jnp.broadcast_to(positives[:, None], (OWN, MARK))
    gain = gain.reshape(D // 128, 128)
    own, scaled, radius = call(
        norm_kernel,
        [
            shaped(OWN, D + MARK, dtype=b16),
            shaped(OWN, D),
            shaped(OWN, 1),
        ],
        "VVV",
        "norm",
    )(features, places, gain)

    mine, own = lax.optimization_barrier((mine, own))
    up, down = along(mine, "y", 1), along(mine, "y", 3)
    far = along(up, "y", 1)

    four = jnp.concatenate([own, other(own, "zl")], axis=0)
    four = jnp.concatenate([four, across(four, 1)], axis=0)
    rows, student, unit, length = call(
        student_kernel,
        [shaped(SIDE, D + MARK, dtype=b16), shaped(SIDE, E, dtype=b16)]
        + [shaped(OWN, E), shaped(OWN, 1)],
        "VVV",
        "student",
        scratch_shapes=[pltpu.VMEM((SIDE, E), f32), pltpu.VMEM((SIDE, 1), f32)],
    )(four, across(four, 3), w_head)
    far, student = lax.optimization_barrier((far, student))
    blocks = [mine, up, down, far]
    blocks += [other(block, "c") for block in blocks]

    message = shaped(SIDE, 2 * E + MARK, dtype=b16)
    teach, expo, terms, col_part, pos_part = call(
        scores_kernel,
        [shaped(wide, E, dtype=b16), shaped(SIDE, wide, dtype=b16), message]
        + [shaped(8, 128), shaped(1, 128)],
        "V" * 10,
        "scores",
    )(student, rows, *blocks)
    col_in = call(cols_kernel, shaped(NCHIP, 8, 128), "VV", "cols")(col_part, other(col_part, "c"))
    col_in = swap(col_in, CHIPS)
    terms, tail = call(
        scaled_kernel,
        [message, shaped(1, 128)],
        "VVVVVV",
        "scaled",
        input_output_aliases={5: 0},
        scratch_shapes=[pltpu.VMEM((SIDE, wide), b16), pltpu.VMEM((8, 128), f32)],
    )(rows, col_in, pos_part, expo, teach, terms)

    terms = swap(terms.reshape(NROW, OWN, 2 * E + MARK), ROW)
    sent, pooled_grad = call(
        rows_kernel,
        [shaped(NROW, 48, 128, dtype=b16), shaped(OWN, D, dtype=b16)],
        "V" * 8,
        "rows",
    )(terms, unit, length, scaled, radius, gain, w_head, tail)
    grad_features = jnp.broadcast_to(pooled_grad[:, None, :], features.shape)

    back = swap(sent, ROW)
    sent = call(head_kernel, shaped(NCHIP, 64, 128, dtype=b16), "VV", "head")(back, rows)
    back = swap(sent, CHIPS)
    last = call(last_kernel, shaped(56, 128), "VA", "last")(back, grad_features)
    grad_head, grad_gain, loss = call(
        out_kernel, [shaped(48, 64), shaped(D // 128, 128), shaped(1, 128)], "VV", "out"
    )(last, other(last, "c"))
    return (loss[0, 0], grad_features, grad_head, grad_gain.reshape(D))


def solution(mesh):
    fine = Mesh(mesh.devices.reshape(4, 4, 4, 2, 2), AXES)
    in_specs = (P(AXES, None, None), P(AXES, None), P(), P(), P(AXES))
    out_specs = (P(), P(AXES, None, None), P(("zh", "y"), ("x", "zl", "c")), P())
    return jax.shard_map(body, mesh=fine, in_specs=in_specs, out_specs=out_specs, check_vma=False)
```

```python
import jax
import jax.numpy as jnp
from jax import lax
from jax.experimental import pallas as pl
from jax.experimental.pallas import tpu as pltpu
from jax.sharding import Mesh, PartitionSpec as P

logit_scale = 64.0
norm_eps = 1e-06

AXES = ("zh", "y", "x", "zl", "c")
ROW = ("x", "zl")
CHIPS = ("zh", "y")

D, E, OWN, WIN = 768, 1024, 32, 32
NROW, NCHIP, NCOL = 8, 16, 32
SIDE = NROW * OWN
HALF = NCHIP * OWN
MARK = 128
CHUNK = 128
BLOCK = 4 * OWN
f32, b16 = jnp.float32, jnp.bfloat16
SPACES = {
    "V": pl.BlockSpec(memory_space=pltpu.VMEM),
    "S": pl.BlockSpec(memory_space=pltpu.SMEM),
    "H": pl.BlockSpec(memory_space=pltpu.HBM),
    "A": pl.BlockSpec(memory_space=pl.ANY),
}
LIMIT = 12 << 20


def shaped(*shape, dtype=f32):
    return jax.ShapeDtypeStruct(shape, dtype)


def unit_rows(raw):
    length = jnp.sqrt(jnp.sum(raw * raw, axis=-1, keepdims=True) + norm_eps)
    return (raw / length, length)


def swap(blocks, axes):
    return lax.all_to_all(blocks, axes, 0, 0, tiled=True)


def spread(block, axes):
    peers = lax.axis_size(axes)
    return swap(jnp.broadcast_to(block[None], (peers,) + block.shape), axes)


def other(block, axis):
    return lax.ppermute(block, axis, [(0, 1), (1, 0)])


def along(block, axis, step):
    return lax.ppermute(block, axis, [(i, (i + step) % 4) for i in range(4)])


def across(block, flip):
    return lax.ppermute(block, "x", [(i, i ^ flip) for i in range(4)])


def halves(value):
    high = value.astype(b16)
    return high, (value - high.astype(f32)).astype(b16)


def product(left, right, left_dim, right_dim):
    dims = (((left_dim,), (right_dim,)), ((), ()))
    return lax.dot_general(left, right, dims, preferred_element_type=f32)


def teacher_kernel(teacher, out):
    out[...] = unit_rows(teacher[...].astype(f32))[0].astype(b16)


def flat(gain):
    return jnp.concatenate([gain[k : k + 1, :] for k in range(D // 128)], axis=1)


def norm_kernel(features, positives, gain, own, scaled, radius):
    for n in range(0, OWN, 8):
        at = slice(n, n + 8)
        pooled = jnp.sum(features[at].astype(f32), axis=1) * (1.0 / WIN)
        size = jnp.sqrt(jnp.mean(pooled * pooled, axis=-1, keepdims=True) + norm_eps)
        radius[at, :] = size
        scaled[at, :] = pooled / size
    own[:, :D] = (scaled[...] * flat(gain)).astype(b16)
    row = lax.broadcasted_iota(jnp.int32, (OWN, OWN), 0)
    col = lax.broadcasted_iota(jnp.int32, (OWN, OWN), 1)
    place = jnp.sum(jnp.where(row == col, positives[...], 0), axis=1, keepdims=True)
    lane = lax.broadcasted_iota(jnp.int32, (OWN, MARK), 1)
    own[:, D:] = jnp.where(lane == 0, place >> 7, place & 127).astype(f32).astype(b16)


def position():
    return [lax.axis_index(a) for a in ("y", "x", "zl", "c", "zh")]


def student_kernel(four, rest, head, rows, student, unit, length, full, sizes):
    where = position()
    x, zl = where[1], where[2]

    def slot(x_, zl_):
        return pl.ds(pl.multiple_of((((x_ + 4) & 3) * 2 + zl_) * OWN, OWN), OWN)

    for k, (ref, start) in enumerate(((four, 0), (four, 64), (rest, 64), (rest, 0))):
        rows[slot(x ^ k, zl), :] = ref[start : start + OWN, :]
        rows[slot(x ^ k, 1 - zl), :] = ref[start + OWN : start + 2 * OWN, :]
    raw = jnp.dot(rows[:, :D], head[...], preferred_element_type=f32)
    full[...], sizes[...] = unit_rows(raw)
    student[...] = full[...].astype(b16)
    unit[...] = full[slot(x, zl), :]
    length[...] = sizes[slot(x, zl), :]


def place(where, k):
    core = where[3] if k < 4 else 1 - where[3]
    y = (where[0] + (0, 3, 1, 2)[k % 4]) & 3
    return core, y


def wanted_mask(marks, where, k):
    core, y = place(where, k)
    marks = marks.astype(f32)
    wanted = marks[:, 0:1] * 128.0 + marks[:, 1:2]
    lane = lax.broadcasted_iota(jnp.int32, (1, BLOCK), 1)
    ids = (((lane >> 5) + where[4]) & 3) * 2048 + (lane & 31)
    ids = ids + y * 512 + where[1] * 128 + where[2] * 64 + core * 32
    return wanted == ids.astype(f32)


def scores_kernel(student, rows, *refs):
    blocks, (teach, expo, terms, col_part, pos_part) = refs[:8], refs[8:]
    where = position()
    for k, block in enumerate(blocks):
        teach[k * BLOCK : (k + 1) * BLOCK, :] = block[...]
    lanes = [jnp.zeros((CHUNK, 128), f32) for _ in range(SIDE // CHUNK)]
    pos = jnp.zeros((1, BLOCK), f32)
    for k in range(0, 8, 2):
        both = product(student[...], teach[k * BLOCK : (k + 2) * BLOCK, :], 1, 1)
        for j in (k, k + 1):
            col = jnp.zeros((1, BLOCK), f32)
            for n in range(SIDE // CHUNK):
                at = slice(n * CHUNK, (n + 1) * CHUNK)
                value = logit_scale * both[at, (j - k) * BLOCK : (j - k + 1) * BLOCK]
                mask = wanted_mask(rows[at, D:], where, j)
                pos = pos + jnp.sum(jnp.where(mask, value, 0.0), axis=0, keepdims=True)
                e = jnp.exp(value)
                expo[at, j * BLOCK : (j + 1) * BLOCK] = e.astype(b16)
                col = col + jnp.sum(e, axis=0, keepdims=True)
                lanes[n] = lanes[n] + e
            core, y = place(where, j)
            col_part[pl.ds(core * 4 + y, 1), :] = col
    col_part[...] = pltpu.roll(col_part[...], where[4] * OWN, 1)
    pos_part[...] = pos
    for n in range(SIDE // CHUNK):
        at = slice(n * CHUNK, (n + 1) * CHUNK)
        high, low = halves(jnp.sum(lanes[n], axis=1, keepdims=True))
        lane = lax.broadcasted_iota(jnp.int32, (CHUNK, MARK), 1)
        terms[at, E : E + MARK] = jnp.where(lane < 64, high.astype(f32), low.astype(f32)).astype(b16)
    terms[:, :E] = product(expo[...], teach[...], 1, 0).astype(b16)


def cols_kernel(mine, pair, sent):
    total = mine[...] + pair[...]
    for g in range(NCHIP):
        sent[g] = total


def scaled_kernel(rows, col_in, pos_part, expo, teach, _, terms, tail, weights, inv):
    where = position()
    cols = jnp.sum(col_in[...], axis=0)
    logs = jnp.sum(jnp.log(cols), axis=0, keepdims=True)
    tail[...] = logs * (1.0 / NCOL) - 2.0 * pos_part[...]
    inv[...] = pltpu.roll(1.0 / cols, ((4 - where[4]) & 3) * OWN, 1)
    for k in range(8):
        core, y = place(where, k)
        scale = inv[pl.ds(core * 4 + y, 1), :]
        at = slice(k * BLOCK, (k + 1) * BLOCK)
        mask = wanted_mask(rows[:, D:], where, k)
        value = expo[:, at].astype(f32) * scale - jnp.where(mask, 2.0, 0.0)
        weights[:, at] = value.astype(b16)
    terms[:, E + MARK :] = product(weights[...], teach[...], 1, 0).astype(b16)


def rows_kernel(terms, unit, length, scaled, radius, gain, head, tail, sent, pooled_grad):
    plain = jnp.zeros((OWN, E), f32)
    weighted = jnp.zeros((OWN, E), f32)
    sums = jnp.zeros((OWN, MARK), f32)
    for s in range(NROW):
        plain = plain + terms[s, :, :E].astype(f32)
        sums = sums + terms[s, :, E : E + MARK].astype(f32)
        weighted = weighted + terms[s, :, E + MARK :].astype(f32)
    row_sums = sums[:, 0:1] + sums[:, 64:65]
    unit_ = unit[...]
    grad_unit = logit_scale * (plain / row_sums + weighted)
    along = jnp.sum(unit_ * grad_unit, axis=-1, keepdims=True)
    grad_raw = ((grad_unit - unit_ * along) / length[...]).astype(b16)
    grad_normed = product(grad_raw, head[...], 1, 1)
    scaled_ = scaled[...]
    gain_part = jnp.sum(grad_normed * scaled_, axis=0, keepdims=True)
    loss = jnp.sum(jnp.log(row_sums), axis=0, keepdims=True)
    loss = loss + jnp.sum(tail[...], axis=1, keepdims=True)
    pieces = [gain_part[:, k * 128 : (k + 1) * 128] for k in range(D // 128)]
    pieces += [jnp.broadcast_to(loss, (1, 128)), jnp.zeros((1, 128), f32)]
    extra = jnp.concatenate(halves(jnp.concatenate(pieces, axis=0)), axis=0)
    for s in range(NROW):
        sent[s, :OWN, :] = grad_raw[:, s * 128 : (s + 1) * 128]
        sent[s, OWN:, :] = extra
    spread_gain = grad_normed * flat(gain)
    inner = jnp.mean(spread_gain * scaled_, axis=-1, keepdims=True)
    grad = (spread_gain - scaled_ * inner) / radius[...]
    pooled_grad[...] = (grad / WIN).astype(b16)


def head_kernel(back, rows, sent):
    grad_raw = back[:, :OWN, :].reshape(SIDE, 128)
    head = product(rows[:, :D], grad_raw, 0, 0).astype(b16)
    extra = jnp.sum(back[:, OWN : OWN + 8, :].astype(f32), axis=0)
    extra = extra + jnp.sum(back[:, OWN + 8 :, :].astype(f32), axis=0)
    extra = jnp.concatenate(halves(extra), axis=0)
    for g in range(NCHIP):
        sent[g, :48, :] = head[g * 48 : (g + 1) * 48, :]
        sent[g, 48:, :] = extra


def last_kernel(back, _, out):
    total = jnp.sum(back[...].astype(f32), axis=0)
    out[:48, :] = total[:48]
    out[48:, :] = total[48:56] + total[56:]


def out_kernel(mine, pair, head, gain, loss):
    total = mine[...] + pair[...]
    head[...] = jnp.where(position()[3] == 0, total[:48, :64], total[:48, 64:])
    gain[...] = total[48 : 48 + D // 128, :]
    loss[...] = total[54:55, :] * (1.0 / (2.0 * OWN * NROW * NCOL))


def call(kernel, out, ins, name, outs=None, limit=LIMIT, **options):
    out_specs = [SPACES[k] for k in outs or "V" * (len(out) if isinstance(out, list) else 1)]
    return pl.pallas_call(
        kernel,
        out_shape=out,
        in_specs=[SPACES[k] for k in ins],
        out_specs=out_specs if isinstance(out, list) else out_specs[0],
        compiler_params=pltpu.CompilerParams(vmem_limit_bytes=limit),
        name=name,
        **options,
    )


def body(features, teacher, gain, w_head, positives):
    wide = 2 * HALF

    mine = call(teacher_kernel, shaped(OWN, E, dtype=b16), "V", "teacher")(teacher)
    mine = jnp.concatenate([mine] + [along(mine, "zh", k) for k in (3, 2, 1)], axis=0)

    gain = gain.reshape(D // 128, 128)
    own, scaled, radius = call(
        norm_kernel,
        [
            shaped(OWN, D + MARK, dtype=b16),
            shaped(OWN, D),
            shaped(OWN, 1),
        ],
        "VVV",
        "norm",
    )(features, positives[None], gain)

    mine, own = lax.optimization_barrier((mine, own))
    up, down = along(mine, "y", 1), along(mine, "y", 3)
    far = along(up, "y", 1)

    four = jnp.concatenate([own, other(own, "zl")], axis=0)
    four = jnp.concatenate([four, across(four, 1)], axis=0)
    rest = across(four, 3)
    far, rest = lax.optimization_barrier((far, rest))
    rows, student, unit, length = call(
        student_kernel,
        [shaped(SIDE, D + MARK, dtype=b16), shaped(SIDE, E, dtype=b16)]
        + [shaped(OWN, E), shaped(OWN, 1)],
        "VVV",
        "student",
        scratch_shapes=[pltpu.VMEM((SIDE, E), f32), pltpu.VMEM((SIDE, 1), f32)],
    )(four, rest, w_head)
    blocks = [mine, up, down, far]
    blocks += [other(block, "c") for block in blocks]

    message = shaped(SIDE, 2 * E + MARK, dtype=b16)
    teach, expo, terms, col_part, pos_part = call(
        scores_kernel,
        [shaped(wide, E, dtype=b16), shaped(SIDE, wide, dtype=b16), message]
        + [shaped(8, 128), shaped(1, 128)],
        "V" * 10,
        "scores",
    )(student, rows, *blocks)
    col_in = call(cols_kernel, shaped(NCHIP, 8, 128), "VV", "cols")(col_part, other(col_part, "c"))
    col_in = swap(col_in, CHIPS)
    terms, tail = call(
        scaled_kernel,
        [message, shaped(1, 128)],
        "VVVVVV",
        "scaled",
        input_output_aliases={5: 0},
        scratch_shapes=[pltpu.VMEM((SIDE, wide), b16), pltpu.VMEM((8, 128), f32)],
    )(rows, col_in, pos_part, expo, teach, terms)

    terms = swap(terms.reshape(NROW, OWN, 2 * E + MARK), ROW)
    sent, pooled_grad = call(
        rows_kernel,
        [shaped(NROW, 48, 128, dtype=b16), shaped(OWN, D, dtype=b16)],
        "V" * 8,
        "rows",
    )(terms, unit, length, scaled, radius, gain, w_head, tail)
    grad_features = jnp.broadcast_to(pooled_grad[:, None, :], features.shape)

    back = swap(sent, ROW)
    sent = call(head_kernel, shaped(NCHIP, 64, 128, dtype=b16), "VV", "head")(back, rows)
    back = swap(sent, CHIPS)
    last = call(last_kernel, shaped(56, 128), "VA", "last")(back, grad_features)
    grad_head, grad_gain, loss = call(
        out_kernel, [shaped(48, 64), shaped(D // 128, 128), shaped(1, 128)], "VV", "out"
    )(last, other(last, "c"))
    return (loss[0, 0], grad_features, grad_head, grad_gain.reshape(D))


def solution(mesh):
    fine = Mesh(mesh.devices.reshape(4, 4, 4, 2, 2), AXES)
    in_specs = (P(AXES, None, None), P(AXES, None), P(), P(), P(AXES))
    out_specs = (P(), P(AXES, None, None), P(("zh", "y"), ("x", "zl", "c")), P())
    return jax.shard_map(body, mesh=fine, in_specs=in_specs, out_specs=out_specs, check_vma=False)
```

```python
import jax
import jax.numpy as jnp
from jax import lax
from jax.experimental import pallas as pl
from jax.experimental.pallas import tpu as pltpu
from jax.sharding import Mesh, PartitionSpec as P

logit_scale = 64.0
norm_eps = 1e-06

AXES = ("zh", "y", "x", "zl", "c")
ROW = ("x", "zl")
CHIPS = ("zh", "y")

D, E, OWN, WIN = 768, 1024, 32, 32
NROW, NCHIP, NCOL = 8, 16, 32
SIDE = NROW * OWN
HALF = NCHIP * OWN
MARK = 128
CHUNK = 128
BLOCK = 4 * OWN
f32, b16 = jnp.float32, jnp.bfloat16
SPACES = {
    "V": pl.BlockSpec(memory_space=pltpu.VMEM),
    "S": pl.BlockSpec(memory_space=pltpu.SMEM),
    "H": pl.BlockSpec(memory_space=pltpu.HBM),
    "A": pl.BlockSpec(memory_space=pl.ANY),
}
LIMIT = 12 << 20


def shaped(*shape, dtype=f32):
    return jax.ShapeDtypeStruct(shape, dtype)


def unit_rows(raw):
    length = jnp.sqrt(jnp.sum(raw * raw, axis=-1, keepdims=True) + norm_eps)
    return (raw / length, length)


def swap(blocks, axes):
    return lax.all_to_all(blocks, axes, 0, 0, tiled=True)


def spread(block, axes):
    peers = lax.axis_size(axes)
    return swap(jnp.broadcast_to(block[None], (peers,) + block.shape), axes)


def other(block, axis):
    return lax.ppermute(block, axis, [(0, 1), (1, 0)])


def along(block, axis, step):
    return lax.ppermute(block, axis, [(i, (i + step) % 4) for i in range(4)])


def across(block, flip):
    return lax.ppermute(block, "x", [(i, i ^ flip) for i in range(4)])


def halves(value):
    high = value.astype(b16)
    return high, (value - high.astype(f32)).astype(b16)


def product(left, right, left_dim, right_dim):
    dims = (((left_dim,), (right_dim,)), ((), ()))
    return lax.dot_general(left, right, dims, preferred_element_type=f32)


def teacher_kernel(teacher, out):
    out[...] = unit_rows(teacher[...].astype(f32))[0].astype(b16)


def flat(gain):
    return jnp.concatenate([gain[k : k + 1, :] for k in range(D // 128)], axis=1)


def norm_kernel(features, positives, gain, own, scaled, radius):
    for n in range(0, OWN, 8):
        at = slice(n, n + 8)
        pooled = jnp.sum(features[at].astype(f32), axis=1) * (1.0 / WIN)
        size = jnp.sqrt(jnp.mean(pooled * pooled, axis=-1, keepdims=True) + norm_eps)
        radius[at, :] = size
        scaled[at, :] = pooled / size
    own[:, :D] = (scaled[...] * flat(gain)).astype(b16)
    row = lax.broadcasted_iota(jnp.int32, (OWN, OWN), 0)
    col = lax.broadcasted_iota(jnp.int32, (OWN, OWN), 1)
    place = jnp.sum(jnp.where(row == col, positives[...], 0), axis=1, keepdims=True)
    lane = lax.broadcasted_iota(jnp.int32, (OWN, MARK), 1)
    own[:, D:] = jnp.where(lane == 0, place >> 7, place & 127).astype(f32).astype(b16)


def position():
    return [lax.axis_index(a) for a in ("y", "x", "zl", "c", "zh")]


def student_kernel(four, rest, head, rows, student, unit, length, full, sizes):
    where = position()
    x, zl = where[1], where[2]

    def slot(x_, zl_):
        return pl.ds(pl.multiple_of((((x_ + 4) & 3) * 2 + zl_) * OWN, OWN), OWN)

    for k, x_ in enumerate((x, x ^ 1, x ^ 3, x ^ 2)):
        at = slice(k * OWN, (k + 1) * OWN)
        rows[slot(x_, zl), :] = four[at, :]
        rows[slot(x_, 1 - zl), :] = rest[at, :]
    raw = jnp.dot(rows[:, :D], head[...], preferred_element_type=f32)
    full[...], sizes[...] = unit_rows(raw)
    student[...] = full[...].astype(b16)
    unit[...] = full[slot(x, zl), :]
    length[...] = sizes[slot(x, zl), :]


def place(where, k):
    core = where[3] if k < 4 else 1 - where[3]
    y = (where[0] + (0, 3, 1, 2)[k % 4]) & 3
    return core, y


def wanted_mask(marks, where, k):
    core, y = place(where, k)
    marks = marks.astype(f32)
    wanted = marks[:, 0:1] * 128.0 + marks[:, 1:2]
    lane = lax.broadcasted_iota(jnp.int32, (1, BLOCK), 1)
    ids = (((lane >> 5) + where[4]) & 3) * 2048 + (lane & 31)
    ids = ids + y * 512 + where[1] * 128 + where[2] * 64 + core * 32
    return wanted == ids.astype(f32)


def scores_kernel(student, rows, *refs):
    blocks, (teach, expo, terms, col_part, pos_part) = refs[:8], refs[8:]
    where = position()
    for k, block in enumerate(blocks):
        teach[k * BLOCK : (k + 1) * BLOCK, :] = block[...]
    lanes = [jnp.zeros((CHUNK, 128), f32) for _ in range(SIDE // CHUNK)]
    pos = jnp.zeros((1, BLOCK), f32)
    for k in range(0, 8, 2):
        both = product(student[...], teach[k * BLOCK : (k + 2) * BLOCK, :], 1, 1)
        for j in (k, k + 1):
            col = jnp.zeros((1, BLOCK), f32)
            for n in range(SIDE // CHUNK):
                at = slice(n * CHUNK, (n + 1) * CHUNK)
                value = logit_scale * both[at, (j - k) * BLOCK : (j - k + 1) * BLOCK]
                mask = wanted_mask(rows[at, D:], where, j)
                pos = pos + jnp.sum(jnp.where(mask, value, 0.0), axis=0, keepdims=True)
                e = jnp.exp(value)
                expo[at, j * BLOCK : (j + 1) * BLOCK] = e.astype(b16)
                col = col + jnp.sum(e, axis=0, keepdims=True)
                lanes[n] = lanes[n] + e
            core, y = place(where, j)
            col_part[pl.ds(core * 4 + y, 1), :] = col
    col_part[...] = pltpu.roll(col_part[...], where[4] * OWN, 1)
    pos_part[...] = pos
    for n in range(SIDE // CHUNK):
        at = slice(n * CHUNK, (n + 1) * CHUNK)
        high, low = halves(jnp.sum(lanes[n], axis=1, keepdims=True))
        lane = lax.broadcasted_iota(jnp.int32, (CHUNK, MARK), 1)
        terms[at, E : E + MARK] = jnp.where(lane < 64, high.astype(f32), low.astype(f32)).astype(b16)
    terms[:, :E] = product(expo[...], teach[...], 1, 0).astype(b16)


def cols_kernel(mine, pair, sent):
    total = mine[...] + pair[...]
    for g in range(NCHIP):
        sent[g] = total


def scaled_kernel(rows, col_in, pos_part, expo, teach, _, terms, tail, weights, inv):
    where = position()
    cols = jnp.sum(col_in[...], axis=0)
    logs = jnp.sum(jnp.log(cols), axis=0, keepdims=True)
    tail[...] = logs * (1.0 / NCOL) - 2.0 * pos_part[...]
    inv[...] = pltpu.roll(1.0 / cols, ((4 - where[4]) & 3) * OWN, 1)
    for k in range(8):
        core, y = place(where, k)
        scale = inv[pl.ds(core * 4 + y, 1), :]
        at = slice(k * BLOCK, (k + 1) * BLOCK)
        mask = wanted_mask(rows[:, D:], where, k)
        value = expo[:, at].astype(f32) * scale - jnp.where(mask, 2.0, 0.0)
        weights[:, at] = value.astype(b16)
    terms[:, E + MARK :] = product(weights[...], teach[...], 1, 0).astype(b16)


def rows_kernel(terms, unit, length, scaled, radius, gain, head, tail, sent, pooled_grad):
    plain = jnp.zeros((OWN, E), f32)
    weighted = jnp.zeros((OWN, E), f32)
    sums = jnp.zeros((OWN, MARK), f32)
    for s in range(NROW):
        plain = plain + terms[s, :, :E].astype(f32)
        sums = sums + terms[s, :, E : E + MARK].astype(f32)
        weighted = weighted + terms[s, :, E + MARK :].astype(f32)
    row_sums = sums[:, 0:1] + sums[:, 64:65]
    unit_ = unit[...]
    grad_unit = logit_scale * (plain / row_sums + weighted)
    along = jnp.sum(unit_ * grad_unit, axis=-1, keepdims=True)
    grad_raw = ((grad_unit - unit_ * along) / length[...]).astype(b16)
    grad_normed = product(grad_raw, head[...], 1, 1)
    scaled_ = scaled[...]
    gain_part = jnp.sum(grad_normed * scaled_, axis=0, keepdims=True)
    loss = jnp.sum(jnp.log(row_sums), axis=0, keepdims=True)
    loss = loss + jnp.sum(tail[...], axis=1, keepdims=True)
    pieces = [gain_part[:, k * 128 : (k + 1) * 128] for k in range(D // 128)]
    pieces += [jnp.broadcast_to(loss, (1, 128)), jnp.zeros((1, 128), f32)]
    extra = jnp.concatenate(halves(jnp.concatenate(pieces, axis=0)), axis=0)
    for s in range(NROW):
        sent[s, :OWN, :] = grad_raw[:, s * 128 : (s + 1) * 128]
        sent[s, OWN:, :] = extra
    spread_gain = grad_normed * flat(gain)
    inner = jnp.mean(spread_gain * scaled_, axis=-1, keepdims=True)
    grad = (spread_gain - scaled_ * inner) / radius[...]
    pooled_grad[...] = (grad / WIN).astype(b16)


def head_kernel(back, rows, sent):
    grad_raw = back[:, :OWN, :].reshape(SIDE, 128)
    head = product(rows[:, :D], grad_raw, 0, 0).astype(b16)
    extra = jnp.sum(back[:, OWN : OWN + 8, :].astype(f32), axis=0)
    extra = extra + jnp.sum(back[:, OWN + 8 :, :].astype(f32), axis=0)
    extra = jnp.concatenate(halves(extra), axis=0)
    for g in range(NCHIP):
        sent[g, :48, :] = head[g * 48 : (g + 1) * 48, :]
        sent[g, 48:, :] = extra


def last_kernel(back, _, out):
    total = jnp.sum(back[...].astype(f32), axis=0)
    out[:48, :] = total[:48]
    out[48:, :] = total[48:56] + total[56:]


def out_kernel(mine, pair, head, gain, loss):
    total = mine[...] + pair[...]
    head[...] = jnp.where(position()[3] == 0, total[:48, :64], total[:48, 64:])
    gain[...] = total[48 : 48 + D // 128, :]
    loss[...] = total[54:55, :] * (1.0 / (2.0 * OWN * NROW * NCOL))


def call(kernel, out, ins, name, outs=None, limit=LIMIT, **options):
    out_specs = [SPACES[k] for k in outs or "V" * (len(out) if isinstance(out, list) else 1)]
    return pl.pallas_call(
        kernel,
        out_shape=out,
        in_specs=[SPACES[k] for k in ins],
        out_specs=out_specs if isinstance(out, list) else out_specs[0],
        compiler_params=pltpu.CompilerParams(vmem_limit_bytes=limit),
        name=name,
        **options,
    )


def body(features, teacher, gain, w_head, positives):
    wide = 2 * HALF

    mine = call(teacher_kernel, shaped(OWN, E, dtype=b16), "V", "teacher")(teacher)
    mine = jnp.concatenate([mine] + [along(mine, "zh", k) for k in (3, 2, 1)], axis=0)

    gain = gain.reshape(D // 128, 128)
    own, scaled, radius = call(
        norm_kernel,
        [
            shaped(OWN, D + MARK, dtype=b16),
            shaped(OWN, D),
            shaped(OWN, 1),
        ],
        "VVV",
        "norm",
    )(features, positives[None], gain)

    mine, own = lax.optimization_barrier((mine, own))
    up, down = along(mine, "y", 1), along(mine, "y", 3)
    far = along(up, "y", 1)

    four = jnp.concatenate([own, across(own, 1)], axis=0)
    four = jnp.concatenate([four, across(four, 3)], axis=0)
    rest = other(four, "zl")
    far, rest = lax.optimization_barrier((far, rest))
    rows, student, unit, length = call(
        student_kernel,
        [shaped(SIDE, D + MARK, dtype=b16), shaped(SIDE, E, dtype=b16)]
        + [shaped(OWN, E), shaped(OWN, 1)],
        "VVV",
        "student",
        scratch_shapes=[pltpu.VMEM((SIDE, E), f32), pltpu.VMEM((SIDE, 1), f32)],
    )(four, rest, w_head)
    blocks = [mine, up, down, far]
    blocks += [other(block, "c") for block in blocks]

    message = shaped(SIDE, 2 * E + MARK, dtype=b16)
    teach, expo, terms, col_part, pos_part = call(
        scores_kernel,
        [shaped(wide, E, dtype=b16), shaped(SIDE, wide, dtype=b16), message]
        + [shaped(8, 128), shaped(1, 128)],
        "V" * 10,
        "scores",
    )(student, rows, *blocks)
    col_in = call(cols_kernel, shaped(NCHIP, 8, 128), "VV", "cols")(col_part, other(col_part, "c"))
    col_in = swap(col_in, CHIPS)
    terms, tail = call(
        scaled_kernel,
        [message, shaped(1, 128)],
        "VVVVVV",
        "scaled",
        input_output_aliases={5: 0},
        scratch_shapes=[pltpu.VMEM((SIDE, wide), b16), pltpu.VMEM((8, 128), f32)],
    )(rows, col_in, pos_part, expo, teach, terms)

    terms = swap(terms.reshape(NROW, OWN, 2 * E + MARK), ROW)
    sent, pooled_grad = call(
        rows_kernel,
        [shaped(NROW, 48, 128, dtype=b16), shaped(OWN, D, dtype=b16)],
        "V" * 8,
        "rows",
    )(terms, unit, length, scaled, radius, gain, w_head, tail)
    grad_features = jnp.broadcast_to(pooled_grad[:, None, :], features.shape)

    back = swap(sent, ROW)
    sent = call(head_kernel, shaped(NCHIP, 64, 128, dtype=b16), "VV", "head")(back, rows)
    back = swap(sent, CHIPS)
    last = call(last_kernel, shaped(56, 128), "VA", "last")(back, grad_features)
    grad_head, grad_gain, loss = call(
        out_kernel, [shaped(48, 64), shaped(D // 128, 128), shaped(1, 128)], "VV", "out"
    )(last, other(last, "c"))
    return (loss[0, 0], grad_features, grad_head, grad_gain.reshape(D))


def solution(mesh):
    fine = Mesh(mesh.devices.reshape(4, 4, 4, 2, 2), AXES)
    in_specs = (P(AXES, None, None), P(AXES, None), P(), P(), P(AXES))
    out_specs = (P(), P(AXES, None, None), P(("zh", "y"), ("x", "zl", "c")), P())
    return jax.shard_map(body, mesh=fine, in_specs=in_specs, out_specs=out_specs, check_vma=False)
```

```python
import jax
import jax.numpy as jnp
from jax import lax
from jax.experimental import pallas as pl
from jax.experimental.pallas import tpu as pltpu
from jax.sharding import Mesh, PartitionSpec as P

logit_scale = 64.0
norm_eps = 1e-06

AXES = ("zh", "y", "x", "zl", "c")
ROW = ("x", "zl")
CHIPS = ("zh", "y")

D, E, OWN, WIN = 768, 1024, 32, 32
NROW, NCHIP, NCOL = 8, 16, 32
SIDE = NROW * OWN
HALF = NCHIP * OWN
MARK = 128
CHUNK = 128
BLOCK = 4 * OWN
f32, b16 = jnp.float32, jnp.bfloat16
SPACES = {
    "V": pl.BlockSpec(memory_space=pltpu.VMEM),
    "S": pl.BlockSpec(memory_space=pltpu.SMEM),
    "H": pl.BlockSpec(memory_space=pltpu.HBM),
    "A": pl.BlockSpec(memory_space=pl.ANY),
}
LIMIT = 12 << 20


def shaped(*shape, dtype=f32):
    return jax.ShapeDtypeStruct(shape, dtype)


def unit_rows(raw):
    length = jnp.sqrt(jnp.sum(raw * raw, axis=-1, keepdims=True) + norm_eps)
    return (raw / length, length)


def swap(blocks, axes):
    return lax.all_to_all(blocks, axes, 0, 0, tiled=True)


def spread(block, axes):
    peers = lax.axis_size(axes)
    return swap(jnp.broadcast_to(block[None], (peers,) + block.shape), axes)


def other(block, axis):
    return lax.ppermute(block, axis, [(0, 1), (1, 0)])


def along(block, axis, step):
    return lax.ppermute(block, axis, [(i, (i + step) % 4) for i in range(4)])


def across(block, flip):
    return lax.ppermute(block, "x", [(i, i ^ flip) for i in range(4)])


def halves(value):
    high = value.astype(b16)
    return high, (value - high.astype(f32)).astype(b16)


def joined(value):
    return jnp.concatenate([half.astype(f32) for half in halves(value)], axis=0).astype(b16)


def product(left, right, left_dim, right_dim):
    dims = (((left_dim,), (right_dim,)), ((), ()))
    return lax.dot_general(left, right, dims, preferred_element_type=f32)


def teacher_kernel(teacher, out):
    out[...] = unit_rows(teacher[...].astype(f32))[0].astype(b16)


def flat(gain):
    return jnp.concatenate([gain[k : k + 1, :] for k in range(D // 128)], axis=1)


def norm_kernel(features, positives, gain, own, scaled, radius):
    for n in range(0, OWN, 8):
        at = slice(n, n + 8)
        pooled = jnp.sum(features[at].astype(f32), axis=1) * (1.0 / WIN)
        size = jnp.sqrt(jnp.mean(pooled * pooled, axis=-1, keepdims=True) + norm_eps)
        radius[at, :] = size
        scaled[at, :] = pooled / size
    own[:, :D] = (scaled[...] * flat(gain)).astype(b16)
    row = lax.broadcasted_iota(jnp.int32, (OWN, OWN), 0)
    col = lax.broadcasted_iota(jnp.int32, (OWN, OWN), 1)
    place = jnp.sum(jnp.where(row == col, positives[...], 0), axis=1, keepdims=True)
    lane = lax.broadcasted_iota(jnp.int32, (OWN, MARK), 1)
    own[:, D:] = jnp.where(lane == 0, place >> 7, place & 127).astype(f32).astype(b16)


def position():
    return [lax.axis_index(a) for a in ("y", "x", "zl", "c", "zh")]


def student_kernel(four, rest, head, rows, student, unit, length, full, sizes):
    where = position()
    x, zl = where[1], where[2]

    def slot(x_, zl_):
        return pl.ds(pl.multiple_of((((x_ + 4) & 3) * 2 + zl_) * OWN, OWN), OWN)

    for k, x_ in enumerate((x, x ^ 1, x ^ 3, x ^ 2)):
        at = slice(k * OWN, (k + 1) * OWN)
        rows[slot(x_, zl), :] = four[at, :]
        rows[slot(x_, 1 - zl), :] = rest[at, :]
    raw = jnp.dot(rows[:, :D], head[...], preferred_element_type=f32)
    full[...], sizes[...] = unit_rows(raw)
    student[...] = full[...].astype(b16)
    unit[...] = full[slot(x, zl), :]
    length[...] = sizes[slot(x, zl), :]


def place(where, k):
    core = where[3] if k < 4 else 1 - where[3]
    y = (where[0] + (0, 3, 1, 2)[k % 4]) & 3
    return core, y


def wanted_mask(marks, where, k):
    core, y = place(where, k)
    marks = marks.astype(f32)
    wanted = marks[:, 0:1] * 128.0 + marks[:, 1:2]
    lane = lax.broadcasted_iota(jnp.int32, (1, BLOCK), 1)
    ids = (((lane >> 5) + where[4]) & 3) * 2048 + (lane & 31)
    ids = ids + y * 512 + where[1] * 128 + where[2] * 64 + core * 32
    return wanted == ids.astype(f32)


def scores_kernel(student, rows, *refs):
    blocks, (teach, expo, terms, col_part, pos_part) = refs[:8], refs[8:]
    where = position()
    for k, block in enumerate(blocks):
        teach[k * BLOCK : (k + 1) * BLOCK, :] = block[...]
    lanes = [jnp.zeros((CHUNK, 128), f32) for _ in range(SIDE // CHUNK)]
    pos = jnp.zeros((1, BLOCK), f32)
    for k in range(0, 8, 2):
        both = product(student[...], teach[k * BLOCK : (k + 2) * BLOCK, :], 1, 1)
        for j in (k, k + 1):
            col = jnp.zeros((1, BLOCK), f32)
            for n in range(SIDE // CHUNK):
                at = slice(n * CHUNK, (n + 1) * CHUNK)
                value = logit_scale * both[at, (j - k) * BLOCK : (j - k + 1) * BLOCK]
                mask = wanted_mask(rows[at, D:], where, j)
                pos = pos + jnp.sum(jnp.where(mask, value, 0.0), axis=0, keepdims=True)
                e = jnp.exp(value)
                expo[at, j * BLOCK : (j + 1) * BLOCK] = e.astype(b16)
                col = col + jnp.sum(e, axis=0, keepdims=True)
                lanes[n] = lanes[n] + e
            core, y = place(where, j)
            col_part[pl.ds(core * 4 + y, 1), :] = col
    col_part[...] = pltpu.roll(col_part[...], where[4] * OWN, 1)
    pos_part[...] = pos
    for n in range(SIDE // CHUNK):
        at = slice(n * CHUNK, (n + 1) * CHUNK)
        high, low = halves(jnp.sum(lanes[n], axis=1, keepdims=True))
        lane = lax.broadcasted_iota(jnp.int32, (CHUNK, MARK), 1)
        terms[at, E : E + MARK] = jnp.where(lane < 64, high.astype(f32), low.astype(f32)).astype(b16)
    terms[:, :E] = product(expo[...], teach[...], 1, 0).astype(b16)


def cols_kernel(mine, pair, sent):
    total = mine[...] + pair[...]
    for g in range(NCHIP):
        sent[g] = total


def scaled_kernel(rows, col_in, pos_part, expo, teach, _, terms, tail, weights, inv):
    where = position()
    cols = jnp.sum(col_in[...], axis=0)
    logs = jnp.sum(jnp.log(cols), axis=0, keepdims=True)
    tail[...] = logs * (1.0 / NCOL) - 2.0 * pos_part[...]
    inv[...] = pltpu.roll(1.0 / cols, ((4 - where[4]) & 3) * OWN, 1)
    for k in range(8):
        core, y = place(where, k)
        scale = inv[pl.ds(core * 4 + y, 1), :]
        at = slice(k * BLOCK, (k + 1) * BLOCK)
        mask = wanted_mask(rows[:, D:], where, k)
        value = expo[:, at].astype(f32) * scale - jnp.where(mask, 2.0, 0.0)
        weights[:, at] = value.astype(b16)
    terms[:, E + MARK :] = product(weights[...], teach[...], 1, 0).astype(b16)


def rows_kernel(terms, unit, length, scaled, radius, gain, head, tail, sent, pooled_grad):
    plain = jnp.zeros((OWN, E), f32)
    weighted = jnp.zeros((OWN, E), f32)
    sums = jnp.zeros((OWN, MARK), f32)
    for s in range(NROW):
        plain = plain + terms[s, :, :E].astype(f32)
        sums = sums + terms[s, :, E : E + MARK].astype(f32)
        weighted = weighted + terms[s, :, E + MARK :].astype(f32)
    row_sums = sums[:, 0:1] + sums[:, 64:65]
    unit_ = unit[...]
    grad_unit = logit_scale * (plain / row_sums + weighted)
    along = jnp.sum(unit_ * grad_unit, axis=-1, keepdims=True)
    grad_raw = ((grad_unit - unit_ * along) / length[...]).astype(b16)
    grad_normed = product(grad_raw, head[...], 1, 1)
    scaled_ = scaled[...]
    gain_part = jnp.sum(grad_normed * scaled_, axis=0, keepdims=True)
    loss = jnp.sum(jnp.log(row_sums), axis=0, keepdims=True)
    loss = loss + jnp.sum(tail[...], axis=1, keepdims=True)
    pieces = [gain_part[:, k * 128 : (k + 1) * 128] for k in range(D // 128)]
    pieces += [jnp.broadcast_to(loss, (1, 128)), jnp.zeros((1, 128), f32)]
    extra = joined(jnp.concatenate(pieces, axis=0))
    for s in range(NROW):
        sent[s, :OWN, :] = grad_raw[:, s * 128 : (s + 1) * 128]
        sent[s, OWN:, :] = extra
    spread_gain = grad_normed * flat(gain)
    inner = jnp.mean(spread_gain * scaled_, axis=-1, keepdims=True)
    grad = (spread_gain - scaled_ * inner) / radius[...]
    pooled_grad[...] = (grad / WIN).astype(b16)


def head_kernel(back, rows, sent):
    grad_raw = back[:, :OWN, :].reshape(SIDE, 128)
    head = product(rows[:, :D], grad_raw, 0, 0).astype(b16)
    extra = jnp.sum(back[:, OWN:, :].astype(f32), axis=0)
    extra = joined(extra[:8] + extra[8:])
    for g in range(NCHIP):
        sent[g, :48, :] = head[g * 48 : (g + 1) * 48, :]
        sent[g, 48:, :] = extra


def last_kernel(back, _, out):
    total = jnp.sum(back[...].astype(f32), axis=0)
    out[:48, :] = total[:48]
    out[48:, :] = total[48:56] + total[56:]


def out_kernel(mine, pair, head, gain, loss):
    total = mine[...] + pair[...]
    head[...] = jnp.where(position()[3] == 0, total[:48, :64], total[:48, 64:])
    gain[...] = total[48 : 48 + D // 128, :]
    loss[...] = total[54:55, :] * (1.0 / (2.0 * OWN * NROW * NCOL))


def call(kernel, out, ins, name, outs=None, limit=LIMIT, **options):
    out_specs = [SPACES[k] for k in outs or "V" * (len(out) if isinstance(out, list) else 1)]
    return pl.pallas_call(
        kernel,
        out_shape=out,
        in_specs=[SPACES[k] for k in ins],
        out_specs=out_specs if isinstance(out, list) else out_specs[0],
        compiler_params=pltpu.CompilerParams(vmem_limit_bytes=limit),
        name=name,
        **options,
    )


def body(features, teacher, gain, w_head, positives):
    wide = 2 * HALF

    mine = call(teacher_kernel, shaped(OWN, E, dtype=b16), "V", "teacher")(teacher)
    mine = jnp.concatenate([mine] + [along(mine, "zh", k) for k in (3, 2, 1)], axis=0)

    gain = gain.reshape(D // 128, 128)
    own, scaled, radius = call(
        norm_kernel,
        [
            shaped(OWN, D + MARK, dtype=b16),
            shaped(OWN, D),
            shaped(OWN, 1),
        ],
        "VVV",
        "norm",
    )(features, positives[None], gain)

    mine, own = lax.optimization_barrier((mine, own))
    up, down = along(mine, "y", 1), along(mine, "y", 3)
    far = along(up, "y", 1)

    four = jnp.concatenate([own, across(own, 1)], axis=0)
    four = jnp.concatenate([four, across(four, 3)], axis=0)
    rest = other(four, "zl")
    far, rest = lax.optimization_barrier((far, rest))
    rows, student, unit, length = call(
        student_kernel,
        [shaped(SIDE, D + MARK, dtype=b16), shaped(SIDE, E, dtype=b16)]
        + [shaped(OWN, E), shaped(OWN, 1)],
        "VVV",
        "student",
        scratch_shapes=[pltpu.VMEM((SIDE, E), f32), pltpu.VMEM((SIDE, 1), f32)],
    )(four, rest, w_head)
    blocks = [mine, up, down, far]
    blocks += [other(block, "c") for block in blocks]

    message = shaped(SIDE, 2 * E + MARK, dtype=b16)
    teach, expo, terms, col_part, pos_part = call(
        scores_kernel,
        [shaped(wide, E, dtype=b16), shaped(SIDE, wide, dtype=b16), message]
        + [shaped(8, 128), shaped(1, 128)],
        "V" * 10,
        "scores",
    )(student, rows, *blocks)
    col_in = call(cols_kernel, shaped(NCHIP, 8, 128), "VV", "cols")(col_part, other(col_part, "c"))
    col_in = swap(col_in, CHIPS)
    terms, tail = call(
        scaled_kernel,
        [message, shaped(1, 128)],
        "VVVVVV",
        "scaled",
        input_output_aliases={5: 0},
        scratch_shapes=[pltpu.VMEM((SIDE, wide), b16), pltpu.VMEM((8, 128), f32)],
    )(rows, col_in, pos_part, expo, teach, terms)

    terms = swap(terms.reshape(NROW, OWN, 2 * E + MARK), ROW)
    sent, pooled_grad = call(
        rows_kernel,
        [shaped(NROW, 48, 128, dtype=b16), shaped(OWN, D, dtype=b16)],
        "V" * 8,
        "rows",
    )(terms, unit, length, scaled, radius, gain, w_head, tail)
    grad_features = jnp.broadcast_to(pooled_grad[:, None, :], features.shape)

    back = swap(sent, ROW)
    sent = call(head_kernel, shaped(NCHIP, 64, 128, dtype=b16), "VV", "head")(back, rows)
    back = swap(sent, CHIPS)
    last = call(last_kernel, shaped(56, 128), "VA", "last")(back, grad_features)
    grad_head, grad_gain, loss = call(
        out_kernel, [shaped(48, 64), shaped(D // 128, 128), shaped(1, 128)], "VV", "out"
    )(last, other(last, "c"))
    return (loss[0, 0], grad_features, grad_head, grad_gain.reshape(D))


def solution(mesh):
    fine = Mesh(mesh.devices.reshape(4, 4, 4, 2, 2), AXES)
    in_specs = (P(AXES, None, None), P(AXES, None), P(), P(), P(AXES))
    out_specs = (P(), P(AXES, None, None), P(("zh", "y"), ("x", "zl", "c")), P())
    return jax.shard_map(body, mesh=fine, in_specs=in_specs, out_specs=out_specs, check_vma=False)
```

```python
import jax
import jax.numpy as jnp
from jax import lax
from jax.experimental import pallas as pl
from jax.experimental.pallas import tpu as pltpu
from jax.sharding import Mesh, PartitionSpec as P

logit_scale = 64.0
norm_eps = 1e-06

AXES = ("zh", "y", "x", "zl", "c")
ROW = ("x", "zl")
CHIPS = ("zh", "y")

D, E, OWN, WIN = 768, 1024, 32, 32
NROW, NCHIP, NCOL = 8, 16, 32
SIDE = NROW * OWN
HALF = NCHIP * OWN
MARK = 128
CHUNK = 128
BLOCK = 4 * OWN
f32, b16 = jnp.float32, jnp.bfloat16
SPACES = {
    "V": pl.BlockSpec(memory_space=pltpu.VMEM),
    "S": pl.BlockSpec(memory_space=pltpu.SMEM),
    "H": pl.BlockSpec(memory_space=pltpu.HBM),
    "A": pl.BlockSpec(memory_space=pl.ANY),
}
LIMIT = 12 << 20


def shaped(*shape, dtype=f32):
    return jax.ShapeDtypeStruct(shape, dtype)


def unit_rows(raw):
    length = jnp.sqrt(jnp.sum(raw * raw, axis=-1, keepdims=True) + norm_eps)
    return (raw / length, length)


def swap(blocks, axes):
    return lax.all_to_all(blocks, axes, 0, 0, tiled=True)


def spread(block, axes):
    peers = lax.axis_size(axes)
    return swap(jnp.broadcast_to(block[None], (peers,) + block.shape), axes)


def other(block, axis):
    return lax.ppermute(block, axis, [(0, 1), (1, 0)])


def along(block, axis, step):
    return lax.ppermute(block, axis, [(i, (i + step) % 4) for i in range(4)])


def across(block, flip):
    return lax.ppermute(block, "x", [(i, i ^ flip) for i in range(4)])


def halves(value):
    high = value.astype(b16)
    return high, (value - high.astype(f32)).astype(b16)


def joined(value):
    return jnp.concatenate([half.astype(f32) for half in halves(value)], axis=0).astype(b16)


def product(left, right, left_dim, right_dim):
    dims = (((left_dim,), (right_dim,)), ((), ()))
    return lax.dot_general(left, right, dims, preferred_element_type=f32)


def teacher_kernel(teacher, out):
    out[...] = unit_rows(teacher[...].astype(f32))[0].astype(b16)


def flat(gain):
    return jnp.concatenate([gain[k : k + 1, :] for k in range(D // 128)], axis=1)


def norm_kernel(features, positives, gain, own, scaled, radius):
    for n in range(0, OWN, 8):
        at = slice(n, n + 8)
        pooled = jnp.sum(features[at].astype(f32), axis=1) * (1.0 / WIN)
        size = jnp.sqrt(jnp.mean(pooled * pooled, axis=-1, keepdims=True) + norm_eps)
        radius[at, :] = size
        scaled[at, :] = pooled / size
    own[:, :D] = (scaled[...] * flat(gain)).astype(b16)
    row = lax.broadcasted_iota(jnp.int32, (OWN, OWN), 0)
    col = lax.broadcasted_iota(jnp.int32, (OWN, OWN), 1)
    place = jnp.sum(jnp.where(row == col, positives[...], 0), axis=1, keepdims=True)
    lane = lax.broadcasted_iota(jnp.int32, (OWN, MARK), 1)
    own[:, D:] = jnp.where(lane == 0, place >> 7, place & 127).astype(f32).astype(b16)


def position():
    return [lax.axis_index(a) for a in ("y", "x", "zl", "c", "zh")]


def student_kernel(four, rest, head, rows, student, unit, length, full, sizes):
    where = position()
    x, zl = where[1], where[2]

    def slot(x_, zl_):
        return pl.ds(pl.multiple_of((((x_ + 4) & 3) * 2 + zl_) * OWN, OWN), OWN)

    for k, x_ in enumerate((x, x ^ 1, x ^ 3, x ^ 2)):
        at = slice(k * OWN, (k + 1) * OWN)
        rows[slot(x_, zl), :] = four[at, :]
        rows[slot(x_, 1 - zl), :] = rest[at, :]
    raw = jnp.dot(rows[:, :D], head[...], preferred_element_type=f32)
    full[...], sizes[...] = unit_rows(raw)
    student[...] = full[...].astype(b16)
    unit[...] = full[slot(x, zl), :]
    length[...] = sizes[slot(x, zl), :]


def place(where, k):
    core = where[3] if k < 4 else 1 - where[3]
    y = (where[0] + (0, 3, 1, 2)[k % 4]) & 3
    return core, y


def wanted_mask(marks, where, k):
    core, y = place(where, k)
    marks = marks.astype(f32)
    wanted = marks[:, 0:1] * 128.0 + marks[:, 1:2]
    lane = lax.broadcasted_iota(jnp.int32, (1, BLOCK), 1)
    ids = (((lane >> 5) + where[4]) & 3) * 2048 + (lane & 31)
    ids = ids + y * 512 + where[1] * 128 + where[2] * 64 + core * 32
    return wanted == ids.astype(f32)


def scores_kernel(student, rows, *refs):
    blocks, (teach, expo, terms, col_part, pos_part) = refs[:8], refs[8:]
    where = position()
    for k, block in enumerate(blocks):
        teach[k * BLOCK : (k + 1) * BLOCK, :] = block[...]
    lanes = [jnp.zeros((CHUNK, 128), f32) for _ in range(SIDE // CHUNK)]
    pos = jnp.zeros((1, BLOCK), f32)
    for k in range(0, 8, 2):
        both = product(student[...], teach[k * BLOCK : (k + 2) * BLOCK, :], 1, 1)
        for j in (k, k + 1):
            col = jnp.zeros((1, BLOCK), f32)
            for n in range(SIDE // CHUNK):
                at = slice(n * CHUNK, (n + 1) * CHUNK)
                value = logit_scale * both[at, (j - k) * BLOCK : (j - k + 1) * BLOCK]
                mask = wanted_mask(rows[at, D:], where, j)
                pos = pos + jnp.sum(jnp.where(mask, value, 0.0), axis=0, keepdims=True)
                e = jnp.exp(value)
                expo[at, j * BLOCK : (j + 1) * BLOCK] = e.astype(b16)
                col = col + jnp.sum(e, axis=0, keepdims=True)
                lanes[n] = lanes[n] + e
            core, y = place(where, j)
            col_part[pl.ds(core * 4 + y, 1), :] = col
    col_part[...] = pltpu.roll(col_part[...], where[4] * OWN, 1)
    pos_part[...] = pos
    for n in range(SIDE // CHUNK):
        at = slice(n * CHUNK, (n + 1) * CHUNK)
        high, low = halves(jnp.sum(lanes[n], axis=1, keepdims=True))
        lane = lax.broadcasted_iota(jnp.int32, (CHUNK, MARK), 1)
        terms[at, E : E + MARK] = jnp.where(lane < 64, high.astype(f32), low.astype(f32)).astype(b16)
    terms[:, :E] = product(expo[...], teach[...], 1, 0).astype(b16)


def cols_kernel(mine, pair, sent):
    total = mine[...] + pair[...]
    for g in range(NCHIP):
        sent[g] = total


def scaled_kernel(rows, col_in, pos_part, expo, teach, _, terms, tail, weights, inv):
    where = position()
    cols = jnp.sum(col_in[...], axis=0)
    logs = jnp.sum(jnp.log(cols), axis=0, keepdims=True)
    tail[...] = logs * (1.0 / NCOL) - 2.0 * pos_part[...]
    inv[...] = pltpu.roll(1.0 / cols, ((4 - where[4]) & 3) * OWN, 1)
    for k in range(8):
        core, y = place(where, k)
        scale = inv[pl.ds(core * 4 + y, 1), :]
        at = slice(k * BLOCK, (k + 1) * BLOCK)
        mask = wanted_mask(rows[:, D:], where, k)
        value = expo[:, at].astype(f32) * scale - jnp.where(mask, 2.0, 0.0)
        weights[:, at] = value.astype(b16)
    terms[:, E + MARK :] = product(weights[...], teach[...], 1, 0).astype(b16)


def rows_kernel(terms, unit, length, scaled, radius, gain, head, tail, sent, pooled_grad):
    plain = jnp.zeros((OWN, E), f32)
    weighted = jnp.zeros((OWN, E), f32)
    sums = jnp.zeros((OWN, MARK), f32)
    for s in range(NROW):
        plain = plain + terms[s, :, :E].astype(f32)
        sums = sums + terms[s, :, E : E + MARK].astype(f32)
        weighted = weighted + terms[s, :, E + MARK :].astype(f32)
    row_sums = sums[:, 0:1] + sums[:, 64:65]
    unit_ = unit[...]
    grad_unit = logit_scale * (plain / row_sums + weighted)
    along = jnp.sum(unit_ * grad_unit, axis=-1, keepdims=True)
    grad_raw = ((grad_unit - unit_ * along) / length[...]).astype(b16)
    grad_normed = product(grad_raw, head[...], 1, 1)
    scaled_ = scaled[...]
    gain_part = jnp.sum(grad_normed * scaled_, axis=0, keepdims=True)
    loss = jnp.sum(jnp.log(row_sums), axis=0, keepdims=True)
    loss = loss + jnp.sum(tail[...], axis=1, keepdims=True)
    pieces = [gain_part[:, k * 128 : (k + 1) * 128] for k in range(D // 128)]
    pieces += [jnp.broadcast_to(loss, (1, 128)), jnp.zeros((1, 128), f32)]
    extra = joined(jnp.concatenate(pieces, axis=0))
    for s in range(NROW):
        sent[s, :OWN, :] = grad_raw[:, s * 128 : (s + 1) * 128]
        sent[s, OWN:, :] = extra
    spread_gain = grad_normed * flat(gain)
    inner = jnp.mean(spread_gain * scaled_, axis=-1, keepdims=True)
    grad = (spread_gain - scaled_ * inner) / radius[...]
    pooled_grad[...] = (grad / WIN).astype(b16)


def head_kernel(back, rows, sent):
    grad_raw = back[:, :OWN, :].reshape(SIDE, 128)
    head = product(rows[:, :D], grad_raw, 0, 0).astype(b16)
    extra = jnp.sum(back[:, OWN:, :].astype(f32), axis=0)
    extra = joined(extra[:8] + extra[8:])
    for g in range(NCHIP):
        sent[g, :48, :] = head[g * 48 : (g + 1) * 48, :]
        sent[g, 48:, :] = extra


def last_kernel(back, _, out):
    total = jnp.sum(back[...].astype(f32), axis=0)
    out[:48, :] = total[:48]
    out[48:, :] = total[48:56] + total[56:]


def out_kernel(mine, pair, head, gain, loss):
    total = mine[...] + pair[...]
    head[...] = jnp.where(position()[3] == 0, total[:48, :64], total[:48, 64:])
    gain[...] = total[48 : 48 + D // 128, :]
    loss[...] = total[54:55, :] * (1.0 / (2.0 * OWN * NROW * NCOL))


def call(kernel, out, ins, name, outs=None, limit=LIMIT, **options):
    out_specs = [SPACES[k] for k in outs or "V" * (len(out) if isinstance(out, list) else 1)]
    return pl.pallas_call(
        kernel,
        out_shape=out,
        in_specs=[SPACES[k] for k in ins],
        out_specs=out_specs if isinstance(out, list) else out_specs[0],
        compiler_params=pltpu.CompilerParams(vmem_limit_bytes=limit),
        name=name,
        **options,
    )


def body(features, teacher, gain, w_head, positives):
    wide = 2 * HALF

    mine = call(teacher_kernel, shaped(OWN, E, dtype=b16), "V", "teacher", limit=56 << 20)(teacher)
    mine = jnp.concatenate([mine] + [along(mine, "zh", k) for k in (3, 2, 1)], axis=0)

    gain = gain.reshape(D // 128, 128)
    own, scaled, radius = call(
        norm_kernel,
        [
            shaped(OWN, D + MARK, dtype=b16),
            shaped(OWN, D),
            shaped(OWN, 1),
        ],
        "VVV",
        "norm",
    )(features, positives[None], gain)

    mine, own = lax.optimization_barrier((mine, own))
    up, down = along(mine, "y", 1), along(mine, "y", 3)
    far = along(up, "y", 1)

    four = jnp.concatenate([own, across(own, 1)], axis=0)
    four = jnp.concatenate([four, across(four, 3)], axis=0)
    rest = other(four, "zl")
    far, rest = lax.optimization_barrier((far, rest))
    rows, student, unit, length = call(
        student_kernel,
        [shaped(SIDE, D + MARK, dtype=b16), shaped(SIDE, E, dtype=b16)]
        + [shaped(OWN, E), shaped(OWN, 1)],
        "VVV",
        "student",
        scratch_shapes=[pltpu.VMEM((SIDE, E), f32), pltpu.VMEM((SIDE, 1), f32)],
    )(four, rest, w_head)
    blocks = [mine, up, down, far]
    blocks += [other(block, "c") for block in blocks]

    message = shaped(SIDE, 2 * E + MARK, dtype=b16)
    teach, expo, terms, col_part, pos_part = call(
        scores_kernel,
        [shaped(wide, E, dtype=b16), shaped(SIDE, wide, dtype=b16), message]
        + [shaped(8, 128), shaped(1, 128)],
        "V" * 10,
        "scores",
    )(student, rows, *blocks)
    col_in = call(cols_kernel, shaped(NCHIP, 8, 128), "VV", "cols")(col_part, other(col_part, "c"))
    col_in = swap(col_in, CHIPS)
    terms, tail = call(
        scaled_kernel,
        [message, shaped(1, 128)],
        "VVVVVV",
        "scaled",
        input_output_aliases={5: 0},
        scratch_shapes=[pltpu.VMEM((SIDE, wide), b16), pltpu.VMEM((8, 128), f32)],
    )(rows, col_in, pos_part, expo, teach, terms)

    terms = swap(terms.reshape(NROW, OWN, 2 * E + MARK), ROW)
    sent, pooled_grad = call(
        rows_kernel,
        [shaped(NROW, 48, 128, dtype=b16), shaped(OWN, D, dtype=b16)],
        "V" * 8,
        "rows",
    )(terms, unit, length, scaled, radius, gain, w_head, tail)
    grad_features = jnp.broadcast_to(pooled_grad[:, None, :], features.shape)

    back = swap(sent, ROW)
    sent = call(head_kernel, shaped(NCHIP, 64, 128, dtype=b16), "VV", "head")(back, rows)
    back = swap(sent, CHIPS)
    last = call(last_kernel, shaped(56, 128), "VA", "last")(back, grad_features)
    grad_head, grad_gain, loss = call(
        out_kernel, [shaped(48, 64), shaped(D // 128, 128), shaped(1, 128)], "VV", "out"
    )(last, other(last, "c"))
    return (loss[0, 0], grad_features, grad_head, grad_gain.reshape(D))


def solution(mesh):
    fine = Mesh(mesh.devices.reshape(4, 4, 4, 2, 2), AXES)
    in_specs = (P(AXES, None, None), P(AXES, None), P(), P(), P(AXES))
    out_specs = (P(), P(AXES, None, None), P(("zh", "y"), ("x", "zl", "c")), P())
    return jax.shard_map(body, mesh=fine, in_specs=in_specs, out_specs=out_specs, check_vma=False)
```

```python
import jax
import jax.numpy as jnp
from jax import lax
from jax.experimental import pallas as pl
from jax.experimental.pallas import tpu as pltpu
from jax.sharding import Mesh, PartitionSpec as P

logit_scale = 64.0
norm_eps = 1e-06

AXES = ("zh", "y", "x", "zl", "c")
ROW = ("x", "zl")
CHIPS = ("zh", "y")

D, E, OWN, WIN = 768, 1024, 32, 32
NROW, NCHIP, NCOL = 8, 16, 32
SIDE = NROW * OWN
HALF = NCHIP * OWN
MARK = 128
CHUNK = 256
BLOCK = 4 * OWN
f32, b16 = jnp.float32, jnp.bfloat16
SPACES = {
    "V": pl.BlockSpec(memory_space=pltpu.VMEM),
    "S": pl.BlockSpec(memory_space=pltpu.SMEM),
    "H": pl.BlockSpec(memory_space=pltpu.HBM),
    "A": pl.BlockSpec(memory_space=pl.ANY),
}
LIMIT = 12 << 20


def shaped(*shape, dtype=f32):
    return jax.ShapeDtypeStruct(shape, dtype)


def unit_rows(raw):
    length = jnp.sqrt(jnp.sum(raw * raw, axis=-1, keepdims=True) + norm_eps)
    return (raw / length, length)


def swap(blocks, axes):
    return lax.all_to_all(blocks, axes, 0, 0, tiled=True)


def spread(block, axes):
    peers = lax.axis_size(axes)
    return swap(jnp.broadcast_to(block[None], (peers,) + block.shape), axes)


def other(block, axis):
    return lax.ppermute(block, axis, [(0, 1), (1, 0)])


def along(block, axis, step):
    return lax.ppermute(block, axis, [(i, (i + step) % 4) for i in range(4)])


def across(block, flip):
    return lax.ppermute(block, "x", [(i, i ^ flip) for i in range(4)])


def halves(value):
    high = value.astype(b16)
    return high, (value - high.astype(f32)).astype(b16)


def joined(value):
    return jnp.concatenate([half.astype(f32) for half in halves(value)], axis=0).astype(b16)


def product(left, right, left_dim, right_dim):
    dims = (((left_dim,), (right_dim,)), ((), ()))
    return lax.dot_general(left, right, dims, preferred_element_type=f32)


def teacher_kernel(teacher, out):
    out[...] = unit_rows(teacher[...].astype(f32))[0].astype(b16)


def flat(gain):
    return jnp.concatenate([gain[k : k + 1, :] for k in range(D // 128)], axis=1)


def norm_kernel(features, positives, gain, own, scaled, radius):
    for n in range(0, OWN, 8):
        at = slice(n, n + 8)
        pooled = jnp.sum(features[at].astype(f32), axis=1) * (1.0 / WIN)
        size = jnp.sqrt(jnp.mean(pooled * pooled, axis=-1, keepdims=True) + norm_eps)
        radius[at, :] = size
        scaled[at, :] = pooled / size
    own[:, :D] = (scaled[...] * flat(gain)).astype(b16)
    row = lax.broadcasted_iota(jnp.int32, (OWN, OWN), 0)
    col = lax.broadcasted_iota(jnp.int32, (OWN, OWN), 1)
    place = jnp.sum(jnp.where(row == col, positives[...], 0), axis=1, keepdims=True)
    lane = lax.broadcasted_iota(jnp.int32, (OWN, MARK), 1)
    own[:, D:] = jnp.where(lane == 0, place >> 7, place & 127).astype(f32).astype(b16)


def position():
    return [lax.axis_index(a) for a in ("y", "x", "zl", "c", "zh")]


def student_kernel(four, rest, head, rows, student, unit, length, full, sizes):
    where = position()
    x, zl = where[1], where[2]

    def slot(x_, zl_):
        return pl.ds(pl.multiple_of((((x_ + 4) & 3) * 2 + zl_) * OWN, OWN), OWN)

    for k, x_ in enumerate((x, x ^ 1, x ^ 3, x ^ 2)):
        at = slice(k * OWN, (k + 1) * OWN)
        rows[slot(x_, zl), :] = four[at, :]
        rows[slot(x_, 1 - zl), :] = rest[at, :]
    raw = jnp.dot(rows[:, :D], head[...], preferred_element_type=f32)
    full[...], sizes[...] = unit_rows(raw)
    student[...] = full[...].astype(b16)
    unit[...] = full[slot(x, zl), :]
    length[...] = sizes[slot(x, zl), :]


def place(where, k):
    core = where[3] if k < 4 else 1 - where[3]
    y = (where[0] + (0, 3, 1, 2)[k % 4]) & 3
    return core, y


def wanted_mask(marks, where, k):
    core, y = place(where, k)
    marks = marks.astype(f32)
    wanted = marks[:, 0:1] * 128.0 + marks[:, 1:2]
    lane = lax.broadcasted_iota(jnp.int32, (1, BLOCK), 1)
    ids = (((lane >> 5) + where[4]) & 3) * 2048 + (lane & 31)
    ids = ids + y * 512 + where[1] * 128 + where[2] * 64 + core * 32
    return wanted == ids.astype(f32)


def scores_kernel(student, rows, *refs):
    blocks, (teach, expo, terms, col_part, pos_part) = refs[:8], refs[8:]
    where = position()
    for k, block in enumerate(blocks):
        teach[k * BLOCK : (k + 1) * BLOCK, :] = block[...]
    lanes = [jnp.zeros((CHUNK, 128), f32) for _ in range(SIDE // CHUNK)]
    pos = jnp.zeros((1, BLOCK), f32)
    for k in range(0, 8, 2):
        both = product(student[...], teach[k * BLOCK : (k + 2) * BLOCK, :], 1, 1)
        for j in (k, k + 1):
            col = jnp.zeros((1, BLOCK), f32)
            for n in range(SIDE // CHUNK):
                at = slice(n * CHUNK, (n + 1) * CHUNK)
                value = logit_scale * both[at, (j - k) * BLOCK : (j - k + 1) * BLOCK]
                mask = wanted_mask(rows[at, D:], where, j)
                pos = pos + jnp.sum(jnp.where(mask, value, 0.0), axis=0, keepdims=True)
                e = jnp.exp(value)
                expo[at, j * BLOCK : (j + 1) * BLOCK] = e.astype(b16)
                col = col + jnp.sum(e, axis=0, keepdims=True)
                lanes[n] = lanes[n] + e
            core, y = place(where, j)
            col_part[pl.ds(core * 4 + y, 1), :] = col
    col_part[...] = pltpu.roll(col_part[...], where[4] * OWN, 1)
    pos_part[...] = pos
    for n in range(SIDE // CHUNK):
        at = slice(n * CHUNK, (n + 1) * CHUNK)
        high, low = halves(jnp.sum(lanes[n], axis=1, keepdims=True))
        lane = lax.broadcasted_iota(jnp.int32, (CHUNK, MARK), 1)
        terms[at, E : E + MARK] = jnp.where(lane < 64, high.astype(f32), low.astype(f32)).astype(b16)
    terms[:, :E] = product(expo[...], teach[...], 1, 0).astype(b16)


def cols_kernel(mine, pair, sent):
    total = mine[...] + pair[...]
    for g in range(NCHIP):
        sent[g] = total


def scaled_kernel(rows, col_in, pos_part, expo, teach, _, terms, tail, weights, inv):
    where = position()
    cols = jnp.sum(col_in[...], axis=0)
    logs = jnp.sum(jnp.log(cols), axis=0, keepdims=True)
    tail[...] = logs * (1.0 / NCOL) - 2.0 * pos_part[...]
    inv[...] = pltpu.roll(1.0 / cols, ((4 - where[4]) & 3) * OWN, 1)
    for k in range(8):
        core, y = place(where, k)
        scale = inv[pl.ds(core * 4 + y, 1), :]
        at = slice(k * BLOCK, (k + 1) * BLOCK)
        mask = wanted_mask(rows[:, D:], where, k)
        value = expo[:, at].astype(f32) * scale - jnp.where(mask, 2.0, 0.0)
        weights[:, at] = value.astype(b16)
    terms[:, E + MARK :] = product(weights[...], teach[...], 1, 0).astype(b16)


def rows_kernel(terms, unit, length, scaled, radius, gain, head, tail, sent, pooled_grad):
    plain = jnp.zeros((OWN, E), f32)
    weighted = jnp.zeros((OWN, E), f32)
    sums = jnp.zeros((OWN, MARK), f32)
    for s in range(NROW):
        plain = plain + terms[s, :, :E].astype(f32)
        sums = sums + terms[s, :, E : E + MARK].astype(f32)
        weighted = weighted + terms[s, :, E + MARK :].astype(f32)
    row_sums = sums[:, 0:1] + sums[:, 64:65]
    unit_ = unit[...]
    grad_unit = logit_scale * (plain / row_sums + weighted)
    along = jnp.sum(unit_ * grad_unit, axis=-1, keepdims=True)
    grad_raw = ((grad_unit - unit_ * along) / length[...]).astype(b16)
    grad_normed = product(grad_raw, head[...], 1, 1)
    scaled_ = scaled[...]
    gain_part = jnp.sum(grad_normed * scaled_, axis=0, keepdims=True)
    loss = jnp.sum(jnp.log(row_sums), axis=0, keepdims=True)
    loss = loss + jnp.sum(tail[...], axis=1, keepdims=True)
    pieces = [gain_part[:, k * 128 : (k + 1) * 128] for k in range(D // 128)]
    pieces += [jnp.broadcast_to(loss, (1, 128)), jnp.zeros((1, 128), f32)]
    extra = joined(jnp.concatenate(pieces, axis=0))
    for s in range(NROW):
        sent[s, :OWN, :] = grad_raw[:, s * 128 : (s + 1) * 128]
        sent[s, OWN:, :] = extra
    spread_gain = grad_normed * flat(gain)
    inner = jnp.mean(spread_gain * scaled_, axis=-1, keepdims=True)
    grad = (spread_gain - scaled_ * inner) / radius[...]
    pooled_grad[...] = (grad / WIN).astype(b16)


def head_kernel(back, rows, sent):
    grad_raw = back[:, :OWN, :].reshape(SIDE, 128)
    head = product(rows[:, :D], grad_raw, 0, 0).astype(b16)
    extra = jnp.sum(back[:, OWN:, :].astype(f32), axis=0)
    extra = joined(extra[:8] + extra[8:])
    for g in range(NCHIP):
        sent[g, :48, :] = head[g * 48 : (g + 1) * 48, :]
        sent[g, 48:, :] = extra


def last_kernel(back, _, out):
    total = jnp.sum(back[...].astype(f32), axis=0)
    out[:48, :] = total[:48]
    out[48:, :] = total[48:56] + total[56:]


def out_kernel(mine, pair, head, gain, loss):
    total = mine[...] + pair[...]
    head[...] = jnp.where(position()[3] == 0, total[:48, :64], total[:48, 64:])
    gain[...] = total[48 : 48 + D // 128, :]
    loss[...] = total[54:55, :] * (1.0 / (2.0 * OWN * NROW * NCOL))


def call(kernel, out, ins, name, outs=None, limit=LIMIT, **options):
    out_specs = [SPACES[k] for k in outs or "V" * (len(out) if isinstance(out, list) else 1)]
    return pl.pallas_call(
        kernel,
        out_shape=out,
        in_specs=[SPACES[k] for k in ins],
        out_specs=out_specs if isinstance(out, list) else out_specs[0],
        compiler_params=pltpu.CompilerParams(vmem_limit_bytes=limit),
        name=name,
        **options,
    )


def body(features, teacher, gain, w_head, positives):
    wide = 2 * HALF

    mine = call(teacher_kernel, shaped(OWN, E, dtype=b16), "V", "teacher")(teacher)
    mine = jnp.concatenate([mine] + [along(mine, "zh", k) for k in (3, 2, 1)], axis=0)

    gain = gain.reshape(D // 128, 128)
    own, scaled, radius = call(
        norm_kernel,
        [
            shaped(OWN, D + MARK, dtype=b16),
            shaped(OWN, D),
            shaped(OWN, 1),
        ],
        "VVV",
        "norm",
    )(features, positives[None], gain)

    mine, own = lax.optimization_barrier((mine, own))
    up, down = along(mine, "y", 1), along(mine, "y", 3)
    far = along(up, "y", 1)

    four = jnp.concatenate([own, across(own, 1)], axis=0)
    four = jnp.concatenate([four, across(four, 3)], axis=0)
    rest = other(four, "zl")
    far, rest = lax.optimization_barrier((far, rest))
    rows, student, unit, length = call(
        student_kernel,
        [shaped(SIDE, D + MARK, dtype=b16), shaped(SIDE, E, dtype=b16)]
        + [shaped(OWN, E), shaped(OWN, 1)],
        "VVV",
        "student",
        scratch_shapes=[pltpu.VMEM((SIDE, E), f32), pltpu.VMEM((SIDE, 1), f32)],
    )(four, rest, w_head)
    blocks = [mine, up, down, far]
    blocks += [other(block, "c") for block in blocks]

    message = shaped(SIDE, 2 * E + MARK, dtype=b16)
    teach, expo, terms, col_part, pos_part = call(
        scores_kernel,
        [shaped(wide, E, dtype=b16), shaped(SIDE, wide, dtype=b16), message]
        + [shaped(8, 128), shaped(1, 128)],
        "V" * 10,
        "scores",
    )(student, rows, *blocks)
    col_in = call(cols_kernel, shaped(NCHIP, 8, 128), "VV", "cols")(col_part, other(col_part, "c"))
    col_in = swap(col_in, CHIPS)
    terms, tail = call(
        scaled_kernel,
        [message, shaped(1, 128)],
        "VVVVVV",
        "scaled",
        input_output_aliases={5: 0},
        scratch_shapes=[pltpu.VMEM((SIDE, wide), b16), pltpu.VMEM((8, 128), f32)],
    )(rows, col_in, pos_part, expo, teach, terms)

    terms = swap(terms.reshape(NROW, OWN, 2 * E + MARK), ROW)
    sent, pooled_grad = call(
        rows_kernel,
        [shaped(NROW, 48, 128, dtype=b16), shaped(OWN, D, dtype=b16)],
        "V" * 8,
        "rows",
    )(terms, unit, length, scaled, radius, gain, w_head, tail)
    grad_features = jnp.broadcast_to(pooled_grad[:, None, :], features.shape)

    back = swap(sent, ROW)
    sent = call(head_kernel, shaped(NCHIP, 64, 128, dtype=b16), "VV", "head")(back, rows)
    back = swap(sent, CHIPS)
    last = call(last_kernel, shaped(56, 128), "VA", "last")(back, grad_features)
    grad_head, grad_gain, loss = call(
        out_kernel, [shaped(48, 64), shaped(D // 128, 128), shaped(1, 128)], "VV", "out"
    )(last, other(last, "c"))
    return (loss[0, 0], grad_features, grad_head, grad_gain.reshape(D))


def solution(mesh):
    fine = Mesh(mesh.devices.reshape(4, 4, 4, 2, 2), AXES)
    in_specs = (P(AXES, None, None), P(AXES, None), P(), P(), P(AXES))
    out_specs = (P(), P(AXES, None, None), P(("zh", "y"), ("x", "zl", "c")), P())
    return jax.shard_map(body, mesh=fine, in_specs=in_specs, out_specs=out_specs, check_vma=False)
```
